32 devices in a mesh: groups: 2 (over x), ctx: 8 (over z, y), head: 2 (over core).
Axes of the slice: x: 2, y: 2, z: 4, core: 2. Of those that a mesh axis runs over, the one named last changes fastest.
Arguments:
- sem_tokens: int32 [2048, 4], P(('groups', 'ctx')), parts along dimension 0, may hold values from 0 to 255
- cand_request: int32 [2048, 1], P(('groups', 'ctx')), parts along dimension 0, may hold values from 0 to 7; in each aligned block of 128 rows (0 to 127, 128 to 255, ...) at most 24 rows name the same one
- hist_lengths: int32 [16], P('groups'), parts along dimension 0, may hold values from 512 to 2048, as said below
- hist_buckets: int32 [16384], P(('groups', 'ctx')), parts along dimension 0, may hold values from 0 to 127
- hist_keys: bfloat16 [16384, 1024], P(('groups', 'ctx'), 'head'), parts along dimension 0, may hold values from -6 to 6
- hist_values: bfloat16 [16384, 1024], P(('groups', 'ctx'), 'head'), parts along dimension 0, may hold values from -18 to 18
- code_table: bfloat16 [1024, 1024], replicated, may hold values from -3 to 3
- proj_in: bfloat16 [1024, 4, 1024], P(None, None, 'head'), may hold values from -0.1875 to 0.1875
- time_bias: float32 [128, 16], P(None, 'head'), may hold values from -6 to 6
- proj_out: bfloat16 [1024, 1024], P('head'), may hold values from -0.1875 to 0.1875
Outputs:
- verified: bfloat16 [2048, 1024], P(('groups', 'ctx'), 'head'), parts along dimension 0
The draws below stay inside these ranges and needn't reach their ends.
There are 2 independent parts, one for each index of `groups`. The reference program is written for one: setup_inputs(seed, part) draws one part's arguments, and reference() takes and returns one part's arrays. A program takes and returns all parts, laid end to end along the dimension named above; an argument that names none is the same for every part. Nothing has to cross between parts.
Inputs may be any that keep to these rules, and one draw needn't show every extreme that they name: `hist_lengths`: every length is a multiple of 512; the lengths sum to 8192; the largest is exactly 2048. `cand_request`: among the candidates of one index of ctx, at most 24 belong to one request.
All inputs are finite; a program needn't handle non-finite values.
Results may differ from the reference program's by a relative error of at most 0.0047.
Values may be sent and summed in bfloat16 or wider, within the bound.
No kernel may reach another device: no remote copies, remote signals or barrier semaphores. Data moves between devices by JAX's collectives and lax.ppermute only.
A program may use at most 64 MiB of HBM per device.

```python
import math
import jax
import jax.numpy as jnp
import numpy as np
from jax import lax

D = 1024
H = 16
DH = 64
LEVELS = 4
CODES = 256
BUCKETS = 128
REQ = 8
CAND_DEV = 128
HIST_DEV = 1024
MOST = 24
CAND = 1024
HIST = 8192
N_CTX = 8


def draw_hist_values(key, part):
    key = jax.random.fold_in(key, 7)
    first_key, second_key, third_key = jax.random.split(key, 3)
    base = jnp.clip(jax.random.normal(first_key, (HIST, D), jnp.float32), -3.0, 3.0)
    columns = jnp.exp(jax.random.uniform(second_key, (1, D), jnp.float32, jnp.log(0.3), jnp.log(3.0)))
    rowwise = jnp.exp(jax.random.uniform(third_key, (HIST, 1), jnp.float32, jnp.log(0.5), jnp.log(2.0)))
    return (base * columns * rowwise).astype(jnp.bfloat16)


def draw_hist_lengths(key, part):
    key = jax.random.fold_in(key, 11)
    cell_key, order_key = jax.random.split(key, 2)
    top_units = N_CTX // 2
    cap_extra = top_units - 1
    extra_total = 2 * N_CTX - top_units - (REQ - 1)
    cell_count = (REQ - 1) * cap_extra
    chosen = jax.random.permutation(cell_key, cell_count)[:extra_total]
    owner = chosen // cap_extra
    extra = jnp.sum((owner[:, None] == jnp.arange(REQ - 1, dtype=jnp.int32)[None, :]).astype(jnp.int32), axis=0)
    units = jnp.concatenate([jnp.full((1,), top_units, jnp.int32), 1 + extra.astype(jnp.int32)])
    units = jax.random.permutation(order_key, units)
    return (units * (HIST_DEV // 2)).astype(jnp.int32)


def place_ends(array, stream_key, least, high):
    shape = array.shape
    spot = [jax.random.randint(jax.random.fold_in(stream_key, axis), (), 0, shape[axis]) for axis in range(len(shape))]
    array = array.at[tuple(spot)].set(least)
    longest = shape.index(max(shape))
    spot[longest] = (spot[longest] + 1) % shape[longest]
    return array.at[tuple(spot)].set(high)


def block_scale(rng, shape, shards, smallest, top_value):
    def one(position, parts):
        draws = jax.random.uniform(jax.random.fold_in(jax.random.fold_in(rng, 6), position), (parts,), jnp.float32, smallest / len(shards), top_value / len(shards))
        return jnp.repeat(jnp.exp(draws), shape[position] // parts).reshape((-1,) + (1,) * (len(shape) - position - 1))

    factor_of = one(*shards[0])
    for cut in shards[1:]:
        factor_of = factor_of * one(*cut)
    return factor_of


def assign_block(rng, own, number, rows, count, top, limit, slope):
    order = jax.random.permutation(rng, count)
    crowded, usual = shares(count, rows * top, limit, slope, True), shares(count, rows * top, limit, slope, False)
    places = jnp.arange(count)

    def named(lengths, turn):
        used = int((lengths > 0).sum())
        fixed = max(1, used // 4)
        moved = fixed + (places - fixed + turn * (used - fixed)) % max(1, count - fixed)
        return jnp.zeros((count,), jnp.int32).at[order[jnp.where(places < fixed, places, moved)]].set(jnp.asarray(lengths, jnp.int32))

    lengths = jnp.where(number % 4 == 0, named(crowded, number // 4), named(usual, number - number // 4 - 1))
    mixed = jax.random.permutation(jax.random.fold_in(own, 3), count)
    giver, receiver = mixed[0:count // 2 * 2:2], mixed[1:count // 2 * 2:2]
    margin = jnp.minimum(lengths[giver] - 1, limit - lengths[receiver]) // 2
    margin = jnp.where((giver == order[0]) | (receiver == order[0]) | (lengths[receiver] == 0), 0, jnp.maximum(margin, 0))
    moved = jax.random.randint(jax.random.fold_in(own, 4), (count // 2,), 0, 1 << 20) % (margin + 1)
    lengths = lengths.at[giver].add(-moved).at[receiver].add(moved)
    members = jnp.searchsorted(jnp.cumsum(lengths), jnp.arange(rows * top), side="right").astype(jnp.int32)
    listing = members.reshape(top, rows).T
    listing = listing[jax.random.permutation(jax.random.fold_in(own, 1), rows)]
    turn = jax.random.randint(jax.random.fold_in(own, 2), (rows, 1), 0, top)
    return jnp.take_along_axis(listing, (jnp.arange(top)[None, :] + turn) % top, axis=1)


def shares(count, total, reach, skew, full):
    loads = [(1 << 20) // math.isqrt(rank ** skew) + 1 for rank in range(1, count + 1)]
    largest = reach if full else min(reach, max(-(-total // count), total * loads[0] // sum(loads)))
    least = 1 if total - largest >= count - 1 else 0
    counts, spare = [largest] + [least] * (count - 1), total - largest - least * (count - 1)
    while spare > 0:
        candidates = [i for i in range(1, count) if counts[i] < largest] or [i for i in range(1, count) if counts[i] < reach]
        pool, remaining = sum([loads[i] for i in candidates]), spare
        for i in candidates:
            addition = min(reach - counts[i], max(1, remaining * loads[i] // pool), spare)
            counts[i] = counts[i] + addition
            spare = spare - addition
    return np.array(counts)


def noise(stream_key, extent, scale, limit, shards=(), kind=jnp.bfloat16):
    factor_of = block_scale(stream_key, extent, shards, -0.22, 0.18) if shards else 1.0
    values = jax.random.normal(stream_key, extent, jnp.float32) * scale * factor_of
    return jnp.minimum(jnp.maximum(values, -limit), limit).astype(kind)


def setup_inputs(seed: int = 0, part: int = 0) -> dict:
    arg_keys = jax.random.split(jax.random.key(seed), 11)
    part_splits = jax.random.split(jax.random.fold_in(arg_keys[10], part), 11)
    sem_tokens = place_ends(jax.random.randint(part_splits[0], (CAND, LEVELS), 0, CODES), jax.random.fold_in(part_splits[0], 1), 0, CODES - 1).astype(jnp.int32)
    cand_request_keys = jax.random.split(jax.random.fold_in(part_splits[1], 1), CAND // CAND_DEV)
    cand_request_turns = jax.random.permutation(jax.random.fold_in(part_splits[1], 3), CAND // CAND_DEV)
    cand_request = jax.vmap(lambda own, number: assign_block(jax.random.fold_in(part_splits[1], 2), own, number, CAND_DEV, REQ, 1, MOST, 2))(cand_request_keys, cand_request_turns).reshape((CAND, 1))
    hist_lengths = draw_hist_lengths(jax.random.fold_in(jax.random.fold_in(arg_keys[10], part), 71), part)
    hist_buckets = place_ends(jax.random.randint(part_splits[3], (HIST,), 0, BUCKETS), jax.random.fold_in(part_splits[3], 1), 0, BUCKETS - 1).astype(jnp.int32)
    hist_keys = noise(part_splits[4], (HIST, D), 1.0, 6.0, ((0, 8), (1, 2)))
    hist_values = draw_hist_values(jax.random.fold_in(jax.random.fold_in(arg_keys[10], part), 71), part)
    code_table = noise(arg_keys[6], (LEVELS * CODES, D), 0.5, 3.0)
    proj_in = noise(arg_keys[7], (D, 4, D), D ** -0.5, 0.1875, ((2, 2),))
    time_bias = noise(arg_keys[8], (BUCKETS, H), 1.0, 6.0, ((1, 2),), jnp.float32)
    proj_out = noise(arg_keys[9], (D, D), D ** -0.5, 0.1875, ((0, 2),))
    return dict(sem_tokens=sem_tokens, cand_request=cand_request, hist_lengths=hist_lengths, hist_buckets=hist_buckets, hist_keys=hist_keys, hist_values=hist_values, code_table=code_table, proj_in=proj_in, time_bias=time_bias, proj_out=proj_out)


def reference(sem_tokens, cand_request, hist_lengths, hist_buckets, hist_keys, hist_values, code_table, proj_in, time_bias, proj_out):
    cand_flat = cand_request[:, 0]
    code_index = sem_tokens + CODES * jnp.arange(LEVELS, dtype=jnp.int32)[None, :]
    embedded = lax.optimization_barrier(jnp.sum(code_table[code_index].astype(jnp.float32), axis=1))
    row_mean = lax.optimization_barrier(jnp.mean(embedded, axis=-1, keepdims=True))
    row_var = lax.optimization_barrier(jnp.mean((embedded - row_mean) ** 2, axis=-1, keepdims=True))
    normed = ((embedded - row_mean) / jnp.sqrt(row_var + 1e-05)).astype(jnp.bfloat16)
    activated = jax.nn.silu(jnp.dot(normed, proj_in.reshape(D, 4 * D), preferred_element_type=jnp.float32)).reshape(CAND, 4, D)
    gate_u = activated[:, 0]
    query = activated[:, 1].astype(jnp.bfloat16)
    self_key = activated[:, 2]
    self_value = activated[:, 3]
    seg_ends = jnp.cumsum(hist_lengths)
    key_seg = lax.optimization_barrier(jnp.sum((jnp.arange(HIST, dtype=jnp.int32)[:, None] >= seg_ends[None, :]).astype(jnp.int32), axis=1))
    key_bias = time_bias[hist_buckets]
    score_scale = DH ** (-0.5)
    key_heads = hist_keys.astype(jnp.float32).reshape(HIST, H, DH)
    value_heads = hist_values.astype(jnp.float32).reshape(HIST, H, DH)
    block_rows = math.gcd(CAND, 64)
    block_count = CAND // block_rows
    query_blocks = query.astype(jnp.float32).reshape(block_count, block_rows, H, DH)
    request_blocks = cand_flat.reshape(block_count, block_rows)

    def attend(packed):
        block_query, block_req = packed
        scores = jnp.einsum('qhe,khe->qhk', block_query, key_heads, precision=lax.Precision.HIGHEST) * score_scale + key_bias.T[None, :, :]
        masked = block_req[:, None] == key_seg[None, :]
        weights = jnp.where(masked[:, None, :], jax.nn.silu(scores), 0.0).astype(jnp.bfloat16)
        weights = lax.optimization_barrier(weights).astype(jnp.float32)
        return jnp.einsum('qhk,khe->qhe', weights, value_heads, precision=lax.Precision.HIGHEST)
    history = lax.map(attend, (query_blocks, request_blocks)).reshape(CAND, H, DH)
    req_lengths = hist_lengths[cand_flat].astype(jnp.float32)
    self_score = lax.optimization_barrier(jnp.sum(query.astype(jnp.float32).reshape(CAND, H, DH) * self_key.reshape(CAND, H, DH), axis=-1)) * score_scale + time_bias[0][None, :]
    attended = history / jnp.sqrt(req_lengths)[:, None, None] + jax.nn.silu(self_score)[:, :, None] * self_value.reshape(CAND, H, DH)
    head_mean = lax.optimization_barrier(jnp.mean(attended, axis=-1, keepdims=True))
    head_var = lax.optimization_barrier(jnp.mean((attended - head_mean) ** 2, axis=-1, keepdims=True))
    normalized = (attended - head_mean) / jnp.sqrt(head_var + 1e-05)
    mixed = (normalized.reshape(CAND, D) * gate_u).astype(jnp.bfloat16)
    verified = embedded + jnp.dot(mixed, proj_out, preferred_element_type=jnp.float32)
    return verified.astype(jnp.bfloat16)
```

```python
import functools

import jax
import jax.numpy as jnp
from jax import lax
from jax.experimental import pallas as pl
from jax.experimental.pallas import tpu as pltpu
from jax.sharding import PartitionSpec as P

MOST = 24
UNIT = 512
ROWS = 8

BF16 = jnp.bfloat16
F32 = jnp.float32
NT = (((1,), (1,)), ((), ()))


def dot(a, b, dims=(((1,), (0,)), ((), ()))):
    return lax.dot_general(a, b, dims, preferred_element_type=F32)


def split_dot(x, b):
    high = x.astype(BF16)
    low = (x - high.astype(F32)).astype(BF16)
    return dot(high, b) + dot(low, b)


def silu(v):
    t = 0.5 * v
    return t + t * jnp.tanh(t)


def iota(shape, dim):
    return lax.broadcasted_iota(jnp.int32, shape, dim)


def upto(size):
    return (iota((size, size), 0) <= iota((size, size), 1)).astype(F32).astype(BF16)


def request_at(position, lens_ref):
    end = lens_ref[0]
    request = jnp.where(position >= end, 1, 0)
    for r in range(1, lens_ref.shape[0]):
        end = end + lens_ref[r]
        request = request + jnp.where(position >= end, 1, 0)
    return request


def embed(tokens, levels, table):
    codes = table.shape[0] // levels
    rows = tokens.shape[0]
    lane = iota((rows, codes), 1).astype(F32)
    hot = jnp.concatenate(
        [jnp.where(lane == tokens[:, l : l + 1], 1.0, 0.0).astype(BF16) for l in range(levels)],
        axis=1,
    )
    return dot(hot, table)


def normalize(embedded):
    width = embedded.shape[1]
    mean = jnp.sum(embedded, axis=1, keepdims=True) * (1.0 / width)
    centred = embedded - mean
    var = jnp.sum(centred * centred, axis=1, keepdims=True) * (1.0 / width)
    return (centred * lax.rsqrt(var + 1e-05)).astype(BF16)


def attend_kernel(
    levels, heads, me_ref, lens_ref, cand_ref, bucket_ref, bias_ref, key_ref, value_ref, table_ref, wq_ref, *rest
):
    owners, _, cand = cand_ref.shape
    outs, (slot_ref, result_ref) = rest[:owners], rest[owners:]
    hist, cols = key_ref.shape
    parts = hist // UNIT
    buckets = bias_ref.shape[1]
    part_rows = owners * MOST
    head_size = cols // heads
    first = me_ref[0] * hist
    order = upto(cand)
    slot = iota((MOST, cand), 0).astype(F32) + 1.0
    requests = cand_ref[:, levels, :]
    tokens = cand_ref[...].astype(F32).astype(BF16)
    for p in range(parts):
        wanted = requests == request_at(first + p * UNIT, lens_ref)
        hot = jnp.where(wanted, 1.0, 0.0)
        rank = jnp.where(wanted, dot(hot.astype(BF16), order), 0.0)
        for k in range(owners):
            pick = jnp.where(slot == rank[k : k + 1, :], 1.0, 0.0).astype(BF16)
            at = p * part_rows + k * MOST
            slot_ref[at : at + MOST, :] = dot(pick, tokens[k], NT)
    query = dot(normalize(embed(slot_ref[...], levels, table_ref[...])), wq_ref[...])
    query = silu(query).astype(BF16) * BF16(0.5 * head_size**-0.5)
    hot = jnp.where(iota((buckets, hist), 0) == bucket_ref[...], 1.0, 0.0).astype(BF16)
    bias = bias_ref[...] * 0.5
    high = bias.astype(BF16)
    low = (bias - high.astype(F32)).astype(BF16)
    bias = dot(high, hot) + dot(low, hot)
    pair = 2 * head_size
    lane = iota((part_rows, pair), 1)
    for p in range(parts):
        rows = slice(p * UNIT, (p + 1) * UNIT)
        for g in range(heads // 2):
            at = slice(g * pair, (g + 1) * pair)
            part = query[p * part_rows : (p + 1) * part_rows, at]
            zero = jnp.zeros_like(part)
            both = jnp.concatenate(
                [jnp.where(lane < head_size, part, zero), jnp.where(lane < head_size, zero, part)], axis=0
            )
            score = dot(both, key_ref[rows, at], NT)
            line = jnp.concatenate(
                [
                    jnp.broadcast_to(bias[2 * g + i : 2 * g + i + 1, rows], (part_rows, UNIT))
                    for i in range(2)
                ],
                axis=0,
            )
            t = score + line
            weight = (t + t * jnp.tanh(t)).astype(BF16)
            summed = dot(weight, value_ref[rows, at])
            kept = jnp.where(lane < head_size, summed[:part_rows], summed[part_rows:])
            for k in range(owners):
                result_ref[k, p * MOST : (p + 1) * MOST, at] = kept[k * MOST : (k + 1) * MOST]
    for k in range(owners):
        outs[k][...] = result_ref[k].astype(BF16)


def own_kernel(
    levels, heads, parts, me_ref, lens_ref, cand_ref, bias_ref, table_ref, win_ref, gate_ref, self_ref, assign_ref, scale_ref, embedded_ref
):
    _, cand = cand_ref.shape
    cols = win_ref.shape[2]
    head_size = cols // heads
    lens_count = lens_ref.shape[0]
    eye = (iota((cand, cand), 0) == iota((cand, cand), 1)).astype(F32).astype(BF16)
    facts = dot(eye, cand_ref[...].astype(F32).astype(BF16), NT)
    embedded = embed(facts, levels, table_ref[...])
    embedded_ref[...] = embedded
    normed = normalize(embedded)
    gate_ref[...] = silu(dot(normed, win_ref[0]))
    query = silu(dot(normed, win_ref[1])).astype(BF16).astype(F32)
    self_key = silu(dot(normed, win_ref[2]))
    self_value = silu(dot(normed, win_ref[3]))
    same = (iota((cols, cols), 0) // head_size == iota((cols, cols), 1) // head_size).astype(F32).astype(BF16)
    spread = (iota((heads, cols), 0) == iota((heads, cols), 1) // head_size).astype(F32)
    first_bias = jnp.sum(spread * bias_ref[:, 0:1], axis=0, keepdims=True)
    score = split_dot(query * self_key, same) * head_size**-0.5 + first_bias
    self_ref[...] = silu(score) * self_value
    request = facts[:, levels : levels + 1]
    other = cand_ref[levels : levels + 1, :].astype(F32)
    before = iota((cand, cand), 0) > iota((cand, cand), 1)
    rank = jnp.sum(jnp.where(jnp.logical_and(request == other, before), 1.0, 0.0), axis=1, keepdims=True)
    slots = assign_ref.shape[1]
    line = iota((1, slots), 1)
    block = line // MOST
    shard = jnp.bitwise_xor(block // parts, me_ref[0])
    slot_request = request_at((shard * parts + block % parts) * UNIT, lens_ref).astype(F32)
    slot_rank = (line % MOST).astype(F32)
    hit = jnp.logical_and(request == slot_request, rank == slot_rank)
    assign_ref[...] = jnp.where(hit, 1.0, 0.0).astype(BF16)
    length = jnp.zeros((cand, 1), F32)
    for r in range(lens_count):
        length = jnp.where(request == float(r), lens_ref[r].astype(F32), length)
    scale_ref[...] = jnp.broadcast_to(lax.rsqrt(length), scale_ref.shape)


def finish_kernel(heads, me_ref, gate_ref, self_ref, assign_ref, scale_ref, embedded_ref, wout_ref, *rest):
    received, (send_ref, keep_ref) = rest[:-2], rest[-2:]
    cols = gate_ref.shape[1]
    head_size = cols // heads
    history = dot(assign_ref[...], jnp.concatenate([r[...] for r in received], axis=0))
    attended = history * scale_ref[:, 0:1] + self_ref[...]
    same = (iota((cols, cols), 0) // head_size == iota((cols, cols), 1) // head_size).astype(F32).astype(BF16)
    centred = attended - split_dot(attended, same) * (1.0 / head_size)
    var = split_dot(centred * centred, same) * (1.0 / head_size)
    mixed = (centred * lax.rsqrt(var + 1e-05) * gate_ref[...]).astype(BF16)
    half = wout_ref.shape[1] // 2
    projected = dot(mixed, wout_ref[...])
    second = me_ref[1] == 1
    send_ref[...] = jnp.where(second, projected[:, :half], projected[:, half:]).astype(BF16)
    keep_ref[...] = jnp.where(
        second, projected[:, half:] + embedded_ref[:, half:], projected[:, :half] + embedded_ref[:, :half]
    )


def full(shape, dtype):
    return jax.ShapeDtypeStruct(shape, dtype)


def body(
    sem_tokens,
    cand_request,
    hist_lengths,
    hist_buckets,
    hist_keys,
    hist_values,
    code_table,
    proj_in,
    time_bias,
    proj_out,
):
    cand, levels = sem_tokens.shape
    hist, cols = hist_keys.shape
    heads = time_bias.shape[1]
    width = code_table.shape[1]
    owners = lax.axis_size("ctx")
    parts = hist // UNIT
    block = parts * MOST
    slots = owners * block
    me = jnp.stack([lax.axis_index("ctx"), lax.axis_index("head")]).astype(jnp.int32)
    payload = jnp.concatenate(
        [sem_tokens.T, cand_request.T, jnp.zeros((ROWS - levels - 1, cand), jnp.int32)], axis=0
    )

    def swap(x, mask):
        return lax.ppermute(x, "ctx", [(i, i ^ mask) for i in range(owners)])

    gathered = payload[None]
    bit = 1
    while bit < owners:
        gathered = jnp.concatenate([gathered, swap(gathered, bit)], axis=0)
        bit *= 2
    weights = jnp.transpose(proj_in, (1, 0, 2))
    bias = time_bias.T
    smem = pl.BlockSpec(memory_space=pltpu.SMEM)
    vmem = pl.BlockSpec(memory_space=pltpu.VMEM)
    sent = pl.pallas_call(
        functools.partial(attend_kernel, levels, heads),
        out_shape=[full((block, cols), BF16)] * owners,
        in_specs=[smem] * 2 + [vmem] * 7,
        out_specs=[vmem] * owners,
        scratch_shapes=[pltpu.VMEM((slots, ROWS), F32), pltpu.VMEM((owners, block, cols), F32)],
        compiler_params=pltpu.CompilerParams(vmem_limit_bytes=40 << 20),
        cost_estimate=pl.CostEstimate(flops=4_000_000_000, bytes_accessed=6 << 20, transcendentals=2_000_000),
        name="attend",
    )(me, hist_lengths, gathered, hist_buckets.reshape(1, hist), bias, hist_keys, hist_values, code_table, weights[1])
    received = [sent[0]] + [swap(sent[m], m) for m in range(1, owners)]
    own = pl.pallas_call(
        functools.partial(own_kernel, levels, heads, parts),
        out_shape=[
            full((cand, cols), F32),
            full((cand, cols), F32),
            full((cand, slots), BF16),
            full((cand, 128), F32),
            full((cand, width), F32),
        ],
        in_specs=[smem] * 2 + [vmem] * 4,
        out_specs=[vmem] * 5,
        compiler_params=pltpu.CompilerParams(vmem_limit_bytes=40 << 20),
        cost_estimate=pl.CostEstimate(flops=2_000_000_000, bytes_accessed=7 << 20, transcendentals=500_000),
        name="own",
    )(me, hist_lengths, payload, bias, code_table, weights)
    send, keep = pl.pallas_call(
        functools.partial(finish_kernel, heads),
        out_shape=[full((cand, width // 2), BF16), full((cand, width // 2), F32)],
        in_specs=[smem] + [vmem] * (6 + owners),
        out_specs=[vmem] * 2,
        compiler_params=pltpu.CompilerParams(vmem_limit_bytes=40 << 20),
        cost_estimate=pl.CostEstimate(flops=1_000_000_000, bytes_accessed=2 << 20, transcendentals=100_000),
        name="finish",
    )(me, *own, proj_out, *received)
    other = lax.ppermute(send, "head", [(0, 1), (1, 0)])
    return (keep + other.astype(F32)).astype(BF16)


def solution(mesh):
    in_specs = (
        P(("groups", "ctx"), None),
        P(("groups", "ctx"), None),
        P("groups"),
        P(("groups", "ctx")),
        P(("groups", "ctx"), "head"),
        P(("groups", "ctx"), "head"),
        P(),
        P(None, None, "head"),
        P(None, "head"),
        P("head", None),
    )
    out_specs = P(("groups", "ctx"), "head")
    return jax.shard_map(body, mesh=mesh, in_specs=in_specs, out_specs=out_specs, check_vma=False)
```

```python
import functools

import jax
import jax.numpy as jnp
from jax import lax
from jax.experimental import pallas as pl
from jax.experimental.pallas import tpu as pltpu
from jax.sharding import PartitionSpec as P

MOST = 24
UNIT = 512
ROWS = 8
LANES = 128

BF16 = jnp.bfloat16
F32 = jnp.float32
NN = (((1,), (0,)), ((), ()))
NT = (((1,), (1,)), ((), ()))


def dot(a, b, dims=NN):
    return lax.dot_general(a, b, dims, preferred_element_type=F32)


def silu(v):
    t = 0.5 * v
    return t + t * jnp.tanh(t)


def iota(shape, dim):
    return lax.broadcasted_iota(jnp.int32, shape, dim)


def ones_where(mask):
    return jnp.where(mask, 1.0, 0.0).astype(BF16)


def head_sums(x, head_size):
    rows, cols = x.shape
    tall = jnp.concatenate([x[:, at : at + LANES] for at in range(0, cols, LANES)], axis=0)
    same = ones_where(iota((LANES, LANES), 0) // head_size == iota((LANES, LANES), 1) // head_size)
    high = tall.astype(BF16)
    low = (tall - high.astype(F32)).astype(BF16)
    sums = dot(high, same) + dot(low, same)
    return jnp.concatenate([sums[at : at + rows] for at in range(0, sums.shape[0], rows)], axis=1)


def request_at(position, lens_ref):
    end = lens_ref[0]
    request = jnp.where(position >= end, 1, 0)
    for r in range(1, lens_ref.shape[0]):
        end = end + lens_ref[r]
        request = request + jnp.where(position >= end, 1, 0)
    return request


def embed(tokens, levels, table):
    codes = table.shape[0] // levels
    lane = iota((tokens.shape[0], codes), 1).astype(F32)
    hot = jnp.concatenate([ones_where(lane == tokens[:, l : l + 1]) for l in range(levels)], axis=1)
    return dot(hot, table)


def normalize(embedded):
    width = embedded.shape[1]
    mean = jnp.sum(embedded, axis=1, keepdims=True) * (1.0 / width)
    centred = embedded - mean
    var = jnp.sum(centred * centred, axis=1, keepdims=True) * (1.0 / width)
    return (centred * lax.rsqrt(var + 1e-05)).astype(BF16)


def slot_queries(parts, levels, scale, me_ref, lens_ref, cand_ref, table_ref, wq_ref, slot_ref):
    owners, _, cand = cand_ref.shape
    first = me_ref[0] * parts * UNIT
    order = ones_where(iota((cand, cand), 0) <= iota((cand, cand), 1))
    slot = iota((MOST, cand), 0).astype(F32) + 1.0
    requests = jnp.concatenate([cand_ref[:, levels, :]] * parts, axis=0)
    line = iota(requests.shape, 0) // owners
    target = jnp.zeros(requests.shape, jnp.int32)
    for p in range(parts):
        target = jnp.where(line == p, request_at(first + p * UNIT, lens_ref), target)
    wanted = requests == target
    rank = jnp.where(wanted, dot(ones_where(wanted), order), 0.0)
    for k in range(owners):
        pick = jnp.concatenate(
            [ones_where(slot == rank[p * owners + k : p * owners + k + 1, :]) for p in range(parts)], axis=0
        )
        facts = dot(pick, cand_ref[k].astype(F32).astype(BF16), NT)
        for p in range(parts):
            at = (p * owners + k) * MOST
            slot_ref[at : at + MOST, :] = facts[p * MOST : (p + 1) * MOST]
    query = dot(normalize(embed(slot_ref[...], levels, table_ref[...])), wq_ref[...])
    return silu(query).astype(BF16) * BF16(scale)


def payload_kernel(cand_ref, out_ref):
    out_ref[...] = cand_ref[...]


def prepare_kernel(
    levels, heads, parts, me_ref, lens_ref, cand_ref, bucket_ref, bias_ref, table_ref,
    normed_ref, residual_ref, assign_ref, scale_ref, line_ref, next_ref,
):
    _, cand = cand_ref.shape
    eye = ones_where(iota((cand, cand), 0) == iota((cand, cand), 1))
    facts = dot(eye, cand_ref[...].astype(F32).astype(BF16), NT)
    embedded = embed(facts, levels, table_ref[...])
    half = embedded.shape[1] // 2
    residual_ref[...] = jnp.where(me_ref[1] == 1, embedded[:, half:], embedded[:, :half])
    normed_ref[...] = normalize(embedded)
    buckets = bias_ref.shape[1]
    hot = ones_where(iota((buckets, bucket_ref.shape[1]), 0) == bucket_ref[...])
    bias = bias_ref[...] * 0.5
    high = bias.astype(BF16)
    low = (bias - high.astype(F32)).astype(BF16)
    line_ref[...] = dot(high, hot) + dot(low, hot)
    request = facts[:, levels : levels + 1]
    other = cand_ref[levels : levels + 1, :].astype(F32)
    before = iota((cand, cand), 0) > iota((cand, cand), 1)
    rank = jnp.sum(jnp.where(jnp.logical_and(request == other, before), 1.0, 0.0), axis=1, keepdims=True)
    line = iota((1, assign_ref.shape[1]), 1)
    block = line // MOST
    owners = assign_ref.shape[1] // (parts * MOST)
    shard = jnp.bitwise_xor(owners - 1 - block // parts, me_ref[0])
    slot_request = request_at((shard * parts + block % parts) * UNIT, lens_ref).astype(F32)
    hit = jnp.logical_and(request == slot_request, rank == (line % MOST).astype(F32))
    assign_ref[...] = ones_where(hit)
    length = jnp.zeros((cand, 1), F32)
    for r in range(lens_ref.shape[0]):
        length = jnp.where(request == float(r), lens_ref[r].astype(F32), length)
    scale_ref[...] = jnp.broadcast_to(lax.rsqrt(length), scale_ref.shape)
    next_ref[...] = cand_ref[...]


def own_kernel(heads, cand_ref, bias_ref, normed_ref, win_ref, gate_ref, self_ref, wq_ref, next_ref):
    cols = win_ref.shape[2]
    head_size = cols // heads
    weights = jnp.swapaxes(win_ref[...], 0, 1)
    normed = normed_ref[...]
    wq_ref[...] = weights[1]
    gate_ref[...] = silu(dot(normed, weights[0]))
    query = silu(dot(normed, weights[1])).astype(BF16).astype(F32)
    self_key = silu(dot(normed, weights[2]))
    spread = jnp.where(iota((heads, cols), 0) == iota((heads, cols), 1) // head_size, 1.0, 0.0)
    first_bias = jnp.sum(spread * bias_ref[:, 0:1], axis=0, keepdims=True)
    score = head_sums(query * self_key, head_size) * head_size**-0.5 + first_bias
    self_ref[...] = silu(score) * silu(dot(normed, weights[3]))
    next_ref[...] = cand_ref[...]


def near_kernel(parts, levels, scale, me_ref, lens_ref, cand_ref, table_ref, wq_ref, query_ref, slot_ref):
    query_ref[...] = slot_queries(parts, levels, scale, me_ref, lens_ref, cand_ref, table_ref, wq_ref, slot_ref)


def attend_kernel(
    parts, levels, heads, stack, scale, me_ref, lens_ref, cand_ref, near_ref, line_ref, key_ref, value_ref, table_ref, wq_ref, *rest
):
    far_owners = cand_ref.shape[0]
    owners = 2 * far_owners
    outs, (slot_ref, result_ref) = rest[:owners], rest[owners:]
    far = slot_queries(parts, levels, scale, me_ref, lens_ref, cand_ref, table_ref, wq_ref, slot_ref)
    cols = key_ref.shape[1]
    head_size = cols // heads
    half = far_owners * MOST
    part_rows = owners * MOST
    wide = stack * head_size
    lane = iota((part_rows, wide), 1) // head_size
    for p in range(parts):
        rows = slice(p * UNIT, (p + 1) * UNIT)
        for g in range(heads // stack):
            at = slice(g * wide, (g + 1) * wide)
            part = jnp.concatenate(
                [near_ref[p * half : (p + 1) * half, at], far[p * half : (p + 1) * half, at]], axis=0
            )
            zero = jnp.zeros_like(part)
            stacked = jnp.concatenate([jnp.where(lane == i, part, zero) for i in range(stack)], axis=0)
            score = dot(stacked, key_ref[rows, at], NT)
            line = jnp.concatenate(
                [
                    jnp.broadcast_to(line_ref[stack * g + i : stack * g + i + 1, rows], (part_rows, UNIT))
                    for i in range(stack)
                ],
                axis=0,
            )
            t = score + line
            weight = (t + t * jnp.tanh(t)).astype(BF16)
            summed = dot(weight, value_ref[rows, at])
            kept = summed[:part_rows]
            for i in range(1, stack):
                kept = jnp.where(lane == i, summed[i * part_rows : (i + 1) * part_rows], kept)
            for k in range(owners):
                result_ref[k, p * MOST : (p + 1) * MOST, at] = kept[k * MOST : (k + 1) * MOST]
    for k in range(owners):
        outs[k][...] = result_ref[k].astype(BF16)


def finish_kernel(heads, me_ref, gate_ref, self_ref, assign_ref, scale_ref, residual_ref, wout_ref, *rest):
    received, (send_ref, keep_ref) = rest[:-2], rest[-2:]
    head_size = gate_ref.shape[1] // heads
    history = dot(assign_ref[...], jnp.concatenate([r[...] for r in received], axis=0))
    attended = history * scale_ref[:, 0:1] + self_ref[...]
    centred = attended - head_sums(attended, head_size) * (1.0 / head_size)
    var = head_sums(centred * centred, head_size) * (1.0 / head_size)
    mixed = (centred * lax.rsqrt(var + 1e-05) * gate_ref[...]).astype(BF16)
    half = wout_ref.shape[1] // 2
    projected = dot(mixed, wout_ref[...])
    second = me_ref[1] == 1
    send_ref[...] = jnp.where(second, projected[:, :half], projected[:, half:]).astype(BF16)
    keep_ref[...] = jnp.where(second, projected[:, half:], projected[:, :half]) + residual_ref[...]


def full(shape, dtype):
    return jax.ShapeDtypeStruct(shape, dtype)


def body(
    sem_tokens,
    cand_request,
    hist_lengths,
    hist_buckets,
    hist_keys,
    hist_values,
    code_table,
    proj_in,
    time_bias,
    proj_out,
):
    cand, levels = sem_tokens.shape
    hist, cols = hist_keys.shape
    heads = time_bias.shape[1]
    width = code_table.shape[1]
    owners = lax.axis_size("ctx")
    parts = hist // UNIT
    block = parts * MOST
    slots = owners * block
    stack = 4
    scale = 0.5 * (cols // heads) ** -0.5
    me = jnp.stack([lax.axis_index("ctx"), lax.axis_index("head")]).astype(jnp.int32)
    bias = time_bias.T
    smem = pl.BlockSpec(memory_space=pltpu.SMEM)
    vmem = pl.BlockSpec(memory_space=pltpu.VMEM)

    def swap(x, mask):
        return lax.ppermute(x, "ctx", [(i, i ^ mask) for i in range(owners)])

    def call(kernel, name, flops, out_shape, in_specs, scratch=(), cost=1 << 20):
        return pl.pallas_call(
            kernel,
            out_shape=out_shape,
            in_specs=in_specs,
            out_specs=jax.tree.map(lambda _: vmem, out_shape),
            scratch_shapes=scratch,
            compiler_params=pltpu.CompilerParams(vmem_limit_bytes=(8 + owners) << 20),
            cost_estimate=pl.CostEstimate(flops=flops, bytes_accessed=cost, transcendentals=0),
            name=name,
        )

    payload = jnp.concatenate(
        [sem_tokens.T, cand_request.T, jnp.zeros((ROWS - levels - 1, cand), jnp.int32)], axis=0
    )
    payload = call(
        payload_kernel, "payload", 9_000_000_000, full((ROWS, cand), jnp.int32), [vmem], cost=32 << 20
    )(payload)
    normed, residual, assign, lengths, line, payload_next = call(
        functools.partial(prepare_kernel, levels, heads, parts),
        "prepare",
        8_000_000_000,
        [
            full((cand, width), BF16),
            full((cand, width // 2), F32),
            full((cand, slots), BF16),
            full((cand, LANES), F32),
            full((heads, hist), F32),
            full((ROWS, cand), jnp.int32),
        ],
        [smem] * 2 + [vmem] * 4,
    )(me, hist_lengths, payload, hist_buckets.reshape(1, hist), bias, code_table)
    first = jnp.stack([payload_next, swap(payload, 1)])
    gate, self_term, wq, first_next = call(
        functools.partial(own_kernel, heads),
        "own",
        1_000_000_000,
        [full((cand, cols), F32)] * 2 + [full((width, cols), BF16), full((2, ROWS, cand), jnp.int32)],
        [vmem] * 4,
    )(first, bias, normed, proj_in)
    gathered = [first, jnp.concatenate([first_next, swap(first, 2)], axis=0)]
    bit = 4
    while bit < owners:
        gathered.append(jnp.concatenate([gathered[-1], swap(gathered[-1], bit)], axis=0))
        bit *= 2
    near_cand, far_cand = gathered[-2], gathered[-1][owners // 2 :]
    near = call(
        functools.partial(near_kernel, parts, levels, scale),
        "near",
        1_000_000_000,
        full((slots // 2, cols), BF16),
        [smem] * 2 + [vmem] * 3,
        [pltpu.VMEM((slots // 2, ROWS), F32)],
    )(me, hist_lengths, near_cand, code_table, wq)
    sent = call(
        functools.partial(attend_kernel, parts, levels, heads, stack, scale),
        "attend",
        3_000_000_000,
        [full((block, cols), BF16)] * owners,
        [smem] * 2 + [vmem] * 7,
        [
            pltpu.VMEM((slots // 2, ROWS), F32),
            pltpu.VMEM((owners, block, cols), F32),
        ],
    )(me, hist_lengths, far_cand, near, line, hist_keys, hist_values, code_table, wq)
    received = [swap(sent[m], m) for m in range(owners - 1, 0, -1)] + [sent[0]]
    send, keep = call(
        functools.partial(finish_kernel, heads),
        "finish",
        1_000_000_000,
        [full((cand, width // 2), BF16), full((cand, width // 2), F32)],
        [smem] + [vmem] * (6 + owners),
    )(me, gate, self_term, assign, lengths, residual, proj_out, *received)
    other = lax.ppermute(send, "head", [(0, 1), (1, 0)])
    return (keep + other.astype(F32)).astype(BF16)


def solution(mesh):
    in_specs = (
        P(("groups", "ctx"), None),
        P(("groups", "ctx"), None),
        P("groups"),
        P(("groups", "ctx")),
        P(("groups", "ctx"), "head"),
        P(("groups", "ctx"), "head"),
        P(),
        P(None, None, "head"),
        P(None, "head"),
        P("head", None),
    )
    out_specs = P(("groups", "ctx"), "head")
    return jax.shard_map(body, mesh=mesh, in_specs=in_specs, out_specs=out_specs, check_vma=False)
```

```python
import functools

import jax
import jax.numpy as jnp
from jax import lax
from jax.experimental import pallas as pl
from jax.experimental.pallas import tpu as pltpu
from jax.sharding import PartitionSpec as P

MOST = 24
UNIT = 512
ROWS = 8
LANES = 128

BF16 = jnp.bfloat16
F32 = jnp.float32
NN = (((1,), (0,)), ((), ()))
NT = (((1,), (1,)), ((), ()))


def dot(a, b, dims=NN):
    return lax.dot_general(a, b, dims, preferred_element_type=F32)


def silu(v):
    t = 0.5 * v
    return t + t * jnp.tanh(t)


def iota(shape, dim):
    return lax.broadcasted_iota(jnp.int32, shape, dim)


def ones_where(mask):
    return jnp.where(mask, 1.0, 0.0).astype(BF16)


def head_sums(x, head_size):
    rows, cols = x.shape
    tall = jnp.concatenate([x[:, at : at + LANES] for at in range(0, cols, LANES)], axis=0)
    same = ones_where(iota((LANES, LANES), 0) // head_size == iota((LANES, LANES), 1) // head_size)
    high = tall.astype(BF16)
    low = (tall - high.astype(F32)).astype(BF16)
    sums = dot(high, same) + dot(low, same)
    return jnp.concatenate([sums[at : at + rows] for at in range(0, sums.shape[0], rows)], axis=1)


def request_at(position, lens_ref):
    end = lens_ref[0]
    request = jnp.where(position >= end, 1, 0)
    for r in range(1, lens_ref.shape[0]):
        end = end + lens_ref[r]
        request = request + jnp.where(position >= end, 1, 0)
    return request


def embed(tokens, levels, table):
    codes = table.shape[0] // levels
    lane = iota((tokens.shape[0], codes), 1).astype(F32)
    hot = jnp.concatenate([ones_where(lane == tokens[:, l : l + 1]) for l in range(levels)], axis=1)
    return dot(hot, table)


def normalize(embedded):
    width = embedded.shape[1]
    mean = jnp.sum(embedded, axis=1, keepdims=True) * (1.0 / width)
    centred = embedded - mean
    var = jnp.sum(centred * centred, axis=1, keepdims=True) * (1.0 / width)
    return (centred * lax.rsqrt(var + 1e-05)).astype(BF16)


def slot_queries(parts, levels, scale, me_ref, lens_ref, cand_ref, table_ref, wq_ref, slot_ref):
    owners, _, cand = cand_ref.shape
    first = me_ref[0] * parts * UNIT
    order = ones_where(iota((cand, cand), 0) <= iota((cand, cand), 1))
    slot = iota((MOST, cand), 0).astype(F32) + 1.0
    requests = jnp.concatenate([cand_ref[:, levels, :]] * parts, axis=0)
    line = iota(requests.shape, 0) // owners
    target = jnp.zeros(requests.shape, jnp.int32)
    for p in range(parts):
        target = jnp.where(line == p, request_at(first + p * UNIT, lens_ref), target)
    wanted = requests == target
    rank = jnp.where(wanted, dot(ones_where(wanted), order), 0.0)
    for k in range(owners):
        pick = jnp.concatenate(
            [ones_where(slot == rank[p * owners + k : p * owners + k + 1, :]) for p in range(parts)], axis=0
        )
        facts = dot(pick, cand_ref[k].astype(F32).astype(BF16), NT)
        for p in range(parts):
            at = (p * owners + k) * MOST
            slot_ref[at : at + MOST, :] = facts[p * MOST : (p + 1) * MOST]
    query = dot(normalize(embed(slot_ref[...], levels, table_ref[...])), wq_ref[...])
    return silu(query).astype(BF16) * BF16(scale)


def payload_kernel(cand_ref, out_ref):
    out_ref[...] = cand_ref[...]


def prepare_kernel(
    levels, heads, parts, me_ref, lens_ref, cand_ref, bucket_ref, bias_ref, table_ref,
    normed_ref, residual_ref, assign_ref, scale_ref, line_ref, next_ref,
):
    _, cand = cand_ref.shape
    eye = ones_where(iota((cand, cand), 0) == iota((cand, cand), 1))
    facts = dot(eye, cand_ref[...].astype(F32).astype(BF16), NT)
    embedded = embed(facts, levels, table_ref[...])
    half = embedded.shape[1] // 2
    residual_ref[...] = jnp.where(me_ref[1] == 1, embedded[:, half:], embedded[:, :half])
    normed_ref[...] = normalize(embedded)
    buckets = bias_ref.shape[1]
    hot = ones_where(iota((buckets, bucket_ref.shape[1]), 0) == bucket_ref[...])
    bias = bias_ref[...] * 0.5
    high = bias.astype(BF16)
    low = (bias - high.astype(F32)).astype(BF16)
    line_ref[...] = dot(high, hot) + dot(low, hot)
    request = facts[:, levels : levels + 1]
    other = cand_ref[levels : levels + 1, :].astype(F32)
    before = iota((cand, cand), 0) > iota((cand, cand), 1)
    rank = jnp.sum(jnp.where(jnp.logical_and(request == other, before), 1.0, 0.0), axis=1, keepdims=True)
    line = iota((1, assign_ref.shape[1]), 1)
    block = line // MOST
    owners = assign_ref.shape[1] // (parts * MOST)
    shard = jnp.bitwise_xor(owners - 1 - block // parts, me_ref[0])
    slot_request = request_at((shard * parts + block % parts) * UNIT, lens_ref).astype(F32)
    hit = jnp.logical_and(request == slot_request, rank == (line % MOST).astype(F32))
    assign_ref[...] = ones_where(hit)
    length = jnp.zeros((cand, 1), F32)
    for r in range(lens_ref.shape[0]):
        length = jnp.where(request == float(r), lens_ref[r].astype(F32), length)
    scale_ref[...] = jnp.broadcast_to(lax.rsqrt(length), scale_ref.shape)
    next_ref[...] = cand_ref[...]


def own_kernel(heads, sent_ref, bias_ref, normed_ref, win_ref, gate_ref, self_ref):
    cols = win_ref.shape[2]
    head_size = cols // heads
    weights = jnp.swapaxes(win_ref[...], 0, 1)
    normed = normed_ref[...]
    gate_ref[...] = silu(dot(normed, weights[0]))
    query = silu(dot(normed, weights[1])).astype(BF16).astype(F32)
    self_key = silu(dot(normed, weights[2]))
    spread = jnp.where(iota((heads, cols), 0) == iota((heads, cols), 1) // head_size, 1.0, 0.0)
    first_bias = jnp.sum(spread * bias_ref[:, 0:1], axis=0, keepdims=True)
    score = head_sums(query * self_key, head_size) * head_size**-0.5 + first_bias
    self_ref[...] = silu(score) * silu(dot(normed, weights[3]))


def near_kernel(parts, levels, scale, me_ref, lens_ref, cand_ref, table_ref, win_ref, query_ref, wq_ref, slot_ref):
    wq_ref[...] = jnp.swapaxes(win_ref[...], 0, 1)[1]
    query_ref[...] = slot_queries(parts, levels, scale, me_ref, lens_ref, cand_ref, table_ref, wq_ref, slot_ref)


def attend_kernel(
    parts, levels, heads, stack, scale, me_ref, lens_ref, cand_ref, near_ref, line_ref, key_ref, value_ref, table_ref, wq_ref, *rest
):
    far_owners = cand_ref.shape[0]
    owners = 2 * far_owners
    outs, (slot_ref, result_ref) = rest[:owners], rest[owners:]
    far = slot_queries(parts, levels, scale, me_ref, lens_ref, cand_ref, table_ref, wq_ref, slot_ref)
    cols = key_ref.shape[1]
    head_size = cols // heads
    half = far_owners * MOST
    part_rows = owners * MOST
    wide = stack * head_size
    lane = iota((part_rows, wide), 1) // head_size
    for p in range(parts):
        rows = slice(p * UNIT, (p + 1) * UNIT)
        for g in range(heads // stack):
            at = slice(g * wide, (g + 1) * wide)
            part = jnp.concatenate(
                [near_ref[p * half : (p + 1) * half, at], far[p * half : (p + 1) * half, at]], axis=0
            )
            zero = jnp.zeros_like(part)
            stacked = jnp.concatenate([jnp.where(lane == i, part, zero) for i in range(stack)], axis=0)
            score = dot(stacked, key_ref[rows, at], NT)
            line = jnp.concatenate(
                [
                    jnp.broadcast_to(line_ref[stack * g + i : stack * g + i + 1, rows], (part_rows, UNIT))
                    for i in range(stack)
                ],
                axis=0,
            )
            t = score + line
            weight = (t + t * jnp.tanh(t)).astype(BF16)
            summed = dot(weight, value_ref[rows, at])
            kept = summed[:part_rows]
            for i in range(1, stack):
                kept = jnp.where(lane == i, summed[i * part_rows : (i + 1) * part_rows], kept)
            for k in range(owners):
                result_ref[k, p * MOST : (p + 1) * MOST, at] = kept[k * MOST : (k + 1) * MOST]
    for k in range(owners):
        outs[k][...] = result_ref[k].astype(BF16)


def finish_kernel(heads, me_ref, gate_ref, self_ref, assign_ref, scale_ref, residual_ref, wout_ref, *rest):
    received, (send_ref, keep_ref) = rest[:-2], rest[-2:]
    head_size = gate_ref.shape[1] // heads
    history = dot(assign_ref[...], jnp.concatenate([r[...] for r in received], axis=0))
    attended = history * scale_ref[:, 0:1] + self_ref[...]
    centred = attended - head_sums(attended, head_size) * (1.0 / head_size)
    var = head_sums(centred * centred, head_size) * (1.0 / head_size)
    mixed = (centred * lax.rsqrt(var + 1e-05) * gate_ref[...]).astype(BF16)
    half = wout_ref.shape[1] // 2
    projected = dot(mixed, wout_ref[...])
    second = me_ref[1] == 1
    send_ref[...] = jnp.where(second, projected[:, :half], projected[:, half:]).astype(BF16)
    keep_ref[...] = jnp.where(second, projected[:, half:], projected[:, :half]) + residual_ref[...]


def full(shape, dtype):
    return jax.ShapeDtypeStruct(shape, dtype)


def body(
    sem_tokens,
    cand_request,
    hist_lengths,
    hist_buckets,
    hist_keys,
    hist_values,
    code_table,
    proj_in,
    time_bias,
    proj_out,
):
    cand, levels = sem_tokens.shape
    hist, cols = hist_keys.shape
    heads = time_bias.shape[1]
    width = code_table.shape[1]
    owners = lax.axis_size("ctx")
    parts = hist // UNIT
    block = parts * MOST
    slots = owners * block
    stack = 4
    scale = 0.5 * (cols // heads) ** -0.5
    me = jnp.stack([lax.axis_index("ctx"), lax.axis_index("head")]).astype(jnp.int32)
    bias = time_bias.T
    smem = pl.BlockSpec(memory_space=pltpu.SMEM)
    vmem = pl.BlockSpec(memory_space=pltpu.VMEM)

    def swap(x, mask):
        return lax.ppermute(x, "ctx", [(i, i ^ mask) for i in range(owners)])

    def call(kernel, name, flops, out_shape, in_specs, scratch=(), cost=1 << 20):
        return pl.pallas_call(
            kernel,
            out_shape=out_shape,
            in_specs=in_specs,
            out_specs=jax.tree.map(lambda _: vmem, out_shape),
            scratch_shapes=scratch,
            compiler_params=pltpu.CompilerParams(vmem_limit_bytes=(8 + owners) << 20),
            cost_estimate=pl.CostEstimate(flops=flops, bytes_accessed=cost, transcendentals=0),
            name=name,
        )

    payload = jnp.concatenate(
        [sem_tokens.T, cand_request.T, jnp.zeros((ROWS - levels - 1, cand), jnp.int32)], axis=0
    )
    payload = call(
        payload_kernel, "payload", 9_000_000_000, full((ROWS, cand), jnp.int32), [vmem], cost=32 << 20
    )(payload)
    normed, residual, assign, lengths, line, payload_next = call(
        functools.partial(prepare_kernel, levels, heads, parts),
        "prepare",
        8_000_000_000,
        [
            full((cand, width), BF16),
            full((cand, width // 2), F32),
            full((cand, slots), BF16),
            full((cand, LANES), F32),
            full((heads, hist), F32),
            full((ROWS, cand), jnp.int32),
        ],
        [smem] * 2 + [vmem] * 4,
    )(me, hist_lengths, payload, hist_buckets.reshape(1, hist), bias, code_table)
    gathered = [jnp.stack([payload_next] + [swap(payload, m) for m in (3, 2, 1)][::-1])]
    bit = 4
    while bit < owners:
        gathered.append(jnp.concatenate([gathered[-1], swap(gathered[-1], bit)], axis=0))
        bit *= 2
    near_cand, far_cand = gathered[-2], gathered[-1][owners // 2 :]
    near, wq = call(
        functools.partial(near_kernel, parts, levels, scale),
        "near",
        1_000_000_000,
        [full((slots // 2, cols), BF16), full((width, cols), BF16)],
        [smem] * 2 + [vmem] * 3,
        [pltpu.VMEM((slots // 2, ROWS), F32)],
    )(me, hist_lengths, near_cand, code_table, proj_in)
    sent = call(
        functools.partial(attend_kernel, parts, levels, heads, stack, scale),
        "attend",
        3_000_000_000,
        [full((block, cols), BF16)] * owners,
        [smem] * 2 + [vmem] * 7,
        [
            pltpu.VMEM((slots // 2, ROWS), F32),
            pltpu.VMEM((owners, block, cols), F32),
        ],
    )(me, hist_lengths, far_cand, near, line, hist_keys, hist_values, code_table, wq)
    gate, self_term = call(
        functools.partial(own_kernel, heads),
        "own",
        1_000_000_000,
        [full((cand, cols), F32)] * 2,
        [vmem] * 4,
    )(sent[0], bias, normed, proj_in)
    received = [swap(sent[m], m) for m in range(owners - 1, 0, -1)] + [sent[0]]
    send, keep = call(
        functools.partial(finish_kernel, heads),
        "finish",
        1_000_000_000,
        [full((cand, width // 2), BF16), full((cand, width // 2), F32)],
        [smem] + [vmem] * (6 + owners),
    )(me, gate, self_term, assign, lengths, residual, proj_out, *received)
    other = lax.ppermute(send, "head", [(0, 1), (1, 0)])
    return (keep + other.astype(F32)).astype(BF16)


def solution(mesh):
    in_specs = (
        P(("groups", "ctx"), None),
        P(("groups", "ctx"), None),
        P("groups"),
        P(("groups", "ctx")),
        P(("groups", "ctx"), "head"),
        P(("groups", "ctx"), "head"),
        P(),
        P(None, None, "head"),
        P(None, "head"),
        P("head", None),
    )
    out_specs = P(("groups", "ctx"), "head")
    return jax.shard_map(body, mesh=mesh, in_specs=in_specs, out_specs=out_specs, check_vma=False)
```

```python
import functools

import jax
import jax.numpy as jnp
from jax import lax
from jax.experimental import pallas as pl
from jax.experimental.pallas import tpu as pltpu
from jax.sharding import PartitionSpec as P

MOST = 24
UNIT = 512
ROWS = 8
LANES = 128

BF16 = jnp.bfloat16
F32 = jnp.float32
NN = (((1,), (0,)), ((), ()))
NT = (((1,), (1,)), ((), ()))


def dot(a, b, dims=NN):
    return lax.dot_general(a, b, dims, preferred_element_type=F32)


def silu(v):
    t = 0.5 * v
    return t + t * jnp.tanh(t)


def iota(shape, dim):
    return lax.broadcasted_iota(jnp.int32, shape, dim)


def ones_where(mask):
    return jnp.where(mask, 1.0, 0.0).astype(BF16)


def head_sums(x, head_size):
    rows, cols = x.shape
    tall = jnp.concatenate([x[:, at : at + LANES] for at in range(0, cols, LANES)], axis=0)
    same = ones_where(iota((LANES, LANES), 0) // head_size == iota((LANES, LANES), 1) // head_size)
    high = tall.astype(BF16)
    low = (tall - high.astype(F32)).astype(BF16)
    sums = dot(high, same) + dot(low, same)
    return jnp.concatenate([sums[at : at + rows] for at in range(0, sums.shape[0], rows)], axis=1)


def request_at(position, lens_ref):
    end = lens_ref[0]
    request = jnp.where(position >= end, 1, 0)
    for r in range(1, lens_ref.shape[0]):
        end = end + lens_ref[r]
        request = request + jnp.where(position >= end, 1, 0)
    return request


def embed(tokens, levels, table):
    codes = table.shape[0] // levels
    lane = iota((tokens.shape[0], codes), 1).astype(F32)
    hot = jnp.concatenate([ones_where(lane == tokens[:, l : l + 1]) for l in range(levels)], axis=1)
    return dot(hot, table)


def normalize(embedded):
    width = embedded.shape[1]
    mean = jnp.sum(embedded, axis=1, keepdims=True) * (1.0 / width)
    centred = embedded - mean
    var = jnp.sum(centred * centred, axis=1, keepdims=True) * (1.0 / width)
    return (centred * lax.rsqrt(var + 1e-05)).astype(BF16)


def slot_queries(parts, levels, scale, me_ref, lens_ref, cand_ref, table_ref, wq_ref, slot_ref):
    owners, _, cand = cand_ref.shape
    first = me_ref[0] * parts * UNIT
    order = ones_where(iota((cand, cand), 0) <= iota((cand, cand), 1))
    slot = iota((MOST, cand), 0).astype(F32) + 1.0
    requests = jnp.concatenate([cand_ref[:, levels, :]] * parts, axis=0)
    line = iota(requests.shape, 0) // owners
    target = jnp.zeros(requests.shape, jnp.int32)
    for p in range(parts):
        target = jnp.where(line == p, request_at(first + p * UNIT, lens_ref), target)
    wanted = requests == target
    rank = jnp.where(wanted, dot(ones_where(wanted), order), 0.0)
    for k in range(owners):
        pick = jnp.concatenate(
            [ones_where(slot == rank[p * owners + k : p * owners + k + 1, :]) for p in range(parts)], axis=0
        )
        facts = dot(pick, cand_ref[k].astype(F32).astype(BF16), NT)
        for p in range(parts):
            at = (p * owners + k) * MOST
            slot_ref[at : at + MOST, :] = facts[p * MOST : (p + 1) * MOST]
    query = dot(normalize(embed(slot_ref[...], levels, table_ref[...])), wq_ref[...])
    return silu(query).astype(BF16) * BF16(scale)


def payload_kernel(cand_ref, out_ref):
    out_ref[...] = cand_ref[...]


def prepare_kernel(
    levels, heads, parts, me_ref, lens_ref, cand_ref, bucket_ref, bias_ref, table_ref,
    normed_ref, residual_ref, assign_ref, scale_ref, line_ref, next_ref,
):
    _, cand = cand_ref.shape
    eye = ones_where(iota((cand, cand), 0) == iota((cand, cand), 1))
    facts = dot(eye, cand_ref[...].astype(F32).astype(BF16), NT)
    embedded = embed(facts, levels, table_ref[...])
    half = embedded.shape[1] // 2
    residual_ref[...] = jnp.where(me_ref[1] == 1, embedded[:, half:], embedded[:, :half])
    normed_ref[...] = normalize(embedded)
    buckets = bias_ref.shape[1]
    hot = ones_where(iota((buckets, bucket_ref.shape[1]), 0) == bucket_ref[...])
    bias = bias_ref[...] * 0.5
    high = bias.astype(BF16)
    low = (bias - high.astype(F32)).astype(BF16)
    line_ref[...] = dot(high, hot) + dot(low, hot)
    request = facts[:, levels : levels + 1]
    other = cand_ref[levels : levels + 1, :].astype(F32)
    before = iota((cand, cand), 0) > iota((cand, cand), 1)
    rank = jnp.sum(jnp.where(jnp.logical_and(request == other, before), 1.0, 0.0), axis=1, keepdims=True)
    line = iota((1, assign_ref.shape[1]), 1)
    block = line // MOST
    owners = assign_ref.shape[1] // (parts * MOST)
    shard = jnp.bitwise_xor(owners - 1 - block // parts, me_ref[0])
    slot_request = request_at((shard * parts + block % parts) * UNIT, lens_ref).astype(F32)
    hit = jnp.logical_and(request == slot_request, rank == (line % MOST).astype(F32))
    assign_ref[...] = ones_where(hit)
    length = jnp.zeros((cand, 1), F32)
    for r in range(lens_ref.shape[0]):
        length = jnp.where(request == float(r), lens_ref[r].astype(F32), length)
    scale_ref[...] = jnp.broadcast_to(lax.rsqrt(length), scale_ref.shape)
    next_ref[...] = cand_ref[...]


def own_kernel(
    heads, me_ref, sent_ref, bias_ref, normed_ref, win_ref, wout_ref, gate_ref, self_ref, mine_ref, other_ref
):
    cols = win_ref.shape[2]
    head_size = cols // heads
    weights = jnp.swapaxes(win_ref[...], 0, 1)
    normed = normed_ref[...]
    gate_ref[...] = silu(dot(normed, weights[0]))
    query = silu(dot(normed, weights[1])).astype(BF16).astype(F32)
    self_key = silu(dot(normed, weights[2]))
    spread = jnp.where(iota((heads, cols), 0) == iota((heads, cols), 1) // head_size, 1.0, 0.0)
    first_bias = jnp.sum(spread * bias_ref[:, 0:1], axis=0, keepdims=True)
    score = head_sums(query * self_key, head_size) * head_size**-0.5 + first_bias
    self_ref[...] = silu(score) * silu(dot(normed, weights[3]))
    half = wout_ref.shape[1] // 2
    low, high = wout_ref[:, :half], wout_ref[:, half:]
    second = me_ref[1] == 1
    mine_ref[...] = jnp.where(second, high, low)
    other_ref[...] = jnp.where(second, low, high)


def attend(parts, heads, stack, owners, query, line_ref, key_ref, value_ref, store):
    cols = key_ref.shape[1]
    head_size = cols // heads
    part_rows = owners * MOST
    wide = stack * head_size
    lane = iota((part_rows, wide), 1) // head_size
    for p in range(parts):
        rows = slice(p * UNIT, (p + 1) * UNIT)
        for g in range(heads // stack):
            at = slice(g * wide, (g + 1) * wide)
            part = query[p * part_rows : (p + 1) * part_rows, at]
            zero = jnp.zeros_like(part)
            stacked = jnp.concatenate([jnp.where(lane == i, part, zero) for i in range(stack)], axis=0)
            score = dot(stacked, key_ref[rows, at], NT)
            line = jnp.concatenate(
                [
                    jnp.broadcast_to(line_ref[stack * g + i : stack * g + i + 1, rows], (part_rows, UNIT))
                    for i in range(stack)
                ],
                axis=0,
            )
            t = score + line
            weight = (t + t * jnp.tanh(t)).astype(BF16)
            summed = dot(weight, value_ref[rows, at])
            kept = summed[:part_rows]
            for i in range(1, stack):
                kept = jnp.where(lane == i, summed[i * part_rows : (i + 1) * part_rows], kept)
            for k in range(owners):
                store(k, p, at, kept[k * MOST : (k + 1) * MOST])


def near_kernel(
    parts, levels, heads, stack, scale,
    me_ref, lens_ref, cand_ref, table_ref, win_ref, line_ref, key_ref, value_ref, *rest
):
    owners = cand_ref.shape[0]
    outs, (wq_ref, slot_ref, result_ref) = rest[:owners], rest[owners:]
    wq_ref[...] = jnp.swapaxes(win_ref[...], 0, 1)[1]
    sums_of(
        parts, levels, heads, stack, scale,
        me_ref, lens_ref, cand_ref, table_ref, wq_ref, line_ref, key_ref, value_ref, outs, slot_ref, result_ref,
    )


def far_kernel(
    parts, levels, heads, stack, scale,
    me_ref, lens_ref, cand_ref, table_ref, wq_ref, line_ref, key_ref, value_ref, *rest
):
    owners = cand_ref.shape[0]
    outs, (slot_ref, result_ref) = rest[:owners], rest[owners:]
    sums_of(
        parts, levels, heads, stack, scale,
        me_ref, lens_ref, cand_ref, table_ref, wq_ref, line_ref, key_ref, value_ref, outs, slot_ref, result_ref,
    )


def sums_of(
    parts, levels, heads, stack, scale,
    me_ref, lens_ref, cand_ref, table_ref, wq_ref, line_ref, key_ref, value_ref, outs, slot_ref, result_ref,
):
    owners = cand_ref.shape[0]
    query = slot_queries(parts, levels, scale, me_ref, lens_ref, cand_ref, table_ref, wq_ref, slot_ref)

    def store(k, p, at, value):
        result_ref[k, p * MOST : (p + 1) * MOST, at] = value

    attend(parts, heads, stack, owners, query, line_ref, key_ref, value_ref, store)
    for k in range(owners):
        outs[k][...] = result_ref[k].astype(BF16)


def mix_kernel(heads, turns, gate_ref, self_ref, assign_ref, scale_ref, wout_ref, *rest):
    received, (mixed_ref, send_ref) = rest[:-2], rest[-2:]
    received = [received[turns.index(m)] for m in range(len(turns), 0, -1)] + [received[-1]]
    head_size = gate_ref.shape[1] // heads
    history = dot(assign_ref[...], jnp.concatenate([r[...] for r in received], axis=0))
    attended = history * scale_ref[:, 0:1] + self_ref[...]
    centred = attended - head_sums(attended, head_size) * (1.0 / head_size)
    var = head_sums(centred * centred, head_size) * (1.0 / head_size)
    mixed = (centred * lax.rsqrt(var + 1e-05) * gate_ref[...]).astype(BF16)
    mixed_ref[...] = mixed
    send_ref[...] = dot(mixed, wout_ref[...]).astype(BF16)


def keep_kernel(mixed_ref, residual_ref, wout_ref, keep_ref):
    keep_ref[...] = residual_ref[...] + dot(mixed_ref[...], wout_ref[...])


def full(shape, dtype):
    return jax.ShapeDtypeStruct(shape, dtype)


def body(
    sem_tokens,
    cand_request,
    hist_lengths,
    hist_buckets,
    hist_keys,
    hist_values,
    code_table,
    proj_in,
    time_bias,
    proj_out,
):
    cand, levels = sem_tokens.shape
    hist, cols = hist_keys.shape
    heads = time_bias.shape[1]
    width = code_table.shape[1]
    owners = lax.axis_size("ctx")
    parts = hist // UNIT
    block = parts * MOST
    slots = owners * block
    stack = 4
    scale = 0.5 * (cols // heads) ** -0.5
    me = jnp.stack([lax.axis_index("ctx"), lax.axis_index("head")]).astype(jnp.int32)
    bias = time_bias.T
    smem = pl.BlockSpec(memory_space=pltpu.SMEM)
    vmem = pl.BlockSpec(memory_space=pltpu.VMEM)

    def swap(x, mask):
        return lax.ppermute(x, "ctx", [(i, i ^ mask) for i in range(owners)])

    def call(kernel, name, flops, out_shape, in_specs, scratch=(), cost=1 << 20):
        return pl.pallas_call(
            kernel,
            out_shape=out_shape,
            in_specs=in_specs,
            out_specs=jax.tree.map(lambda _: vmem, out_shape),
            scratch_shapes=scratch,
            compiler_params=pltpu.CompilerParams(vmem_limit_bytes=(8 + owners) << 20),
            cost_estimate=pl.CostEstimate(flops=flops, bytes_accessed=cost, transcendentals=0),
            name=name,
        )

    payload = jnp.concatenate(
        [sem_tokens.T, cand_request.T, jnp.zeros((ROWS - levels - 1, cand), jnp.int32)], axis=0
    )
    payload = call(
        payload_kernel, "payload", 9_000_000_000, full((ROWS, cand), jnp.int32), [vmem], cost=32 << 20
    )(payload)
    normed, residual, assign, lengths, line, payload_next = call(
        functools.partial(prepare_kernel, levels, heads, parts),
        "prepare",
        8_000_000_000,
        [
            full((cand, width), BF16),
            full((cand, width // 2), F32),
            full((cand, slots), BF16),
            full((cand, LANES), F32),
            full((heads, hist), F32),
            full((ROWS, cand), jnp.int32),
        ],
        [smem] * 2 + [vmem] * 4,
    )(me, hist_lengths, payload, hist_buckets.reshape(1, hist), bias, code_table)
    gathered = [jnp.stack([payload_next] + [swap(payload, m) for m in (3, 2, 1)][::-1])]
    bit = 4
    while bit < owners:
        gathered.append(jnp.concatenate([gathered[-1], swap(gathered[-1], bit)], axis=0))
        bit *= 2
    near_cand, far_cand = gathered[-2], gathered[-1][owners // 2 :]
    half = owners // 2
    scratch = [pltpu.VMEM((slots // 2, ROWS), F32), pltpu.VMEM((half, block, cols), F32)]
    *near, wq = call(
        functools.partial(near_kernel, parts, levels, heads, stack, scale),
        "near",
        1_000_000_000,
        [full((block, cols), BF16)] * half + [full((width, cols), BF16)],
        [smem] * 2 + [vmem] * 6,
        scratch,
    )(me, hist_lengths, near_cand, code_table, proj_in, line, hist_keys, hist_values)
    far = call(
        functools.partial(far_kernel, parts, levels, heads, stack, scale),
        "far",
        3_000_000_000,
        [full((block, cols), BF16)] * half,
        [smem] * 2 + [vmem] * 6,
        scratch,
    )(me, hist_lengths, far_cand, code_table, wq, line, hist_keys, hist_values)
    sent = list(lax.optimization_barrier(tuple(near) + tuple(far)))
    gate, self_term, wout_mine, wout_other = call(
        functools.partial(own_kernel, heads),
        "own",
        1_000_000_000,
        [full((cand, cols), F32)] * 2 + [full((cols, width // 2), BF16)] * 2,
        [smem] + [vmem] * 5,
    )(me, sent[0], bias, normed, proj_in, proj_out)
    turns = [4, 7, 6, 5, 3, 2, 1] if owners == 8 else list(range(owners - 1, 0, -1))
    received = [swap(sent[m], m) for m in turns] + [sent[0]]
    mixed, send = call(
        functools.partial(mix_kernel, heads, turns),
        "mix",
        1_000_000_000,
        [full((cand, cols), BF16), full((cand, width // 2), BF16)],
        [vmem] * (5 + owners),
    )(gate, self_term, assign, lengths, wout_other, *received)
    other = lax.ppermute(send, "head", [(0, 1), (1, 0)])
    keep = call(keep_kernel, "keep", 1_000_000, full((cand, width // 2), F32), [vmem] * 3)(
        mixed, residual, wout_mine
    )
    return (keep + other.astype(F32)).astype(BF16)


def solution(mesh):
    in_specs = (
        P(("groups", "ctx"), None),
        P(("groups", "ctx"), None),
        P("groups"),
        P(("groups", "ctx")),
        P(("groups", "ctx"), "head"),
        P(("groups", "ctx"), "head"),
        P(),
        P(None, None, "head"),
        P(None, "head"),
        P("head", None),
    )
    out_specs = P(("groups", "ctx"), "head")
    return jax.shard_map(body, mesh=mesh, in_specs=in_specs, out_specs=out_specs, check_vma=False)
```

```python
import functools

import jax
import jax.numpy as jnp
from jax import lax
from jax.experimental import pallas as pl
from jax.experimental.pallas import tpu as pltpu
from jax.sharding import PartitionSpec as P

MOST = 24
UNIT = 512
ROWS = 8
LANES = 128

BF16 = jnp.bfloat16
F32 = jnp.float32
NN = (((1,), (0,)), ((), ()))
NT = (((1,), (1,)), ((), ()))


def dot(a, b, dims=NN):
    return lax.dot_general(a, b, dims, preferred_element_type=F32)


def silu(v):
    t = 0.5 * v
    return t + t * jnp.tanh(t)


def iota(shape, dim):
    return lax.broadcasted_iota(jnp.int32, shape, dim)


def ones_where(mask):
    return jnp.where(mask, 1.0, 0.0).astype(BF16)


def head_sums(x, head_size):
    rows, cols = x.shape
    tall = jnp.concatenate([x[:, at : at + LANES] for at in range(0, cols, LANES)], axis=0)
    same = ones_where(iota((LANES, LANES), 0) // head_size == iota((LANES, LANES), 1) // head_size)
    high = tall.astype(BF16)
    low = (tall - high.astype(F32)).astype(BF16)
    sums = dot(high, same) + dot(low, same)
    return jnp.concatenate([sums[at : at + rows] for at in range(0, sums.shape[0], rows)], axis=1)


def request_at(position, lens_ref):
    end = lens_ref[0]
    request = jnp.where(position >= end, 1, 0)
    for r in range(1, lens_ref.shape[0]):
        end = end + lens_ref[r]
        request = request + jnp.where(position >= end, 1, 0)
    return request


def embed(tokens, levels, table):
    codes = table.shape[0] // levels
    lane = iota((tokens.shape[0], codes), 1).astype(F32)
    hot = jnp.concatenate([ones_where(lane == tokens[:, l : l + 1]) for l in range(levels)], axis=1)
    return dot(hot, table)


def normalize(embedded):
    width = embedded.shape[1]
    mean = jnp.sum(embedded, axis=1, keepdims=True) * (1.0 / width)
    centred = embedded - mean
    var = jnp.sum(centred * centred, axis=1, keepdims=True) * (1.0 / width)
    return (centred * lax.rsqrt(var + 1e-05)).astype(BF16)


def slot_queries(parts, levels, scale, me_ref, lens_ref, cand_ref, table_ref, wq_ref, slot_ref):
    owners, _, cand = cand_ref.shape
    first = me_ref[0] * parts * UNIT
    order = ones_where(iota((cand, cand), 0) <= iota((cand, cand), 1))
    slot = iota((MOST, cand), 0).astype(F32) + 1.0
    requests = jnp.concatenate([cand_ref[:, levels, :]] * parts, axis=0)
    line = iota(requests.shape, 0) // owners
    target = jnp.zeros(requests.shape, jnp.int32)
    for p in range(parts):
        target = jnp.where(line == p, request_at(first + p * UNIT, lens_ref), target)
    wanted = requests == target
    rank = jnp.where(wanted, dot(ones_where(wanted), order), 0.0)
    for k in range(owners):
        pick = jnp.concatenate(
            [ones_where(slot == rank[p * owners + k : p * owners + k + 1, :]) for p in range(parts)], axis=0
        )
        facts = dot(pick, cand_ref[k].astype(F32).astype(BF16), NT)
        for p in range(parts):
            at = (p * owners + k) * MOST
            slot_ref[at : at + MOST, :] = facts[p * MOST : (p + 1) * MOST]
    query = dot(normalize(embed(slot_ref[...], levels, table_ref[...])), wq_ref[...])
    return silu(query).astype(BF16) * BF16(scale)


def payload_kernel(cand_ref, out_ref):
    out_ref[...] = cand_ref[...]


def prepare_kernel(
    levels, heads, parts, me_ref, lens_ref, cand_ref, bucket_ref, bias_ref, table_ref,
    normed_ref, residual_ref, assign_ref, scale_ref, line_ref, next_ref,
):
    _, cand = cand_ref.shape
    eye = ones_where(iota((cand, cand), 0) == iota((cand, cand), 1))
    facts = dot(eye, cand_ref[...].astype(F32).astype(BF16), NT)
    embedded = embed(facts, levels, table_ref[...])
    half = embedded.shape[1] // 2
    residual_ref[...] = jnp.where(me_ref[1] == 1, embedded[:, half:], embedded[:, :half])
    normed_ref[...] = normalize(embedded)
    buckets = bias_ref.shape[1]
    hot = ones_where(iota((buckets, bucket_ref.shape[1]), 0) == bucket_ref[...])
    bias = bias_ref[...] * 0.5
    high = bias.astype(BF16)
    low = (bias - high.astype(F32)).astype(BF16)
    line_ref[...] = dot(high, hot) + dot(low, hot)
    request = facts[:, levels : levels + 1]
    other = cand_ref[levels : levels + 1, :].astype(F32)
    before = iota((cand, cand), 0) > iota((cand, cand), 1)
    rank = jnp.sum(jnp.where(jnp.logical_and(request == other, before), 1.0, 0.0), axis=1, keepdims=True)
    line = iota((1, assign_ref.shape[1]), 1)
    block = line // MOST
    owners = assign_ref.shape[1] // (parts * MOST)
    shard = jnp.bitwise_xor(owners - 1 - block // parts, me_ref[0])
    slot_request = request_at((shard * parts + block % parts) * UNIT, lens_ref).astype(F32)
    hit = jnp.logical_and(request == slot_request, rank == (line % MOST).astype(F32))
    assign_ref[...] = ones_where(hit)
    length = jnp.zeros((cand, 1), F32)
    for r in range(lens_ref.shape[0]):
        length = jnp.where(request == float(r), lens_ref[r].astype(F32), length)
    scale_ref[...] = jnp.broadcast_to(lax.rsqrt(length), scale_ref.shape)
    next_ref[...] = cand_ref[...]


def own_kernel(
    heads, me_ref, sent_ref, bias_ref, normed_ref, win_ref, wout_ref, gate_ref, self_ref, mine_ref, other_ref
):
    cols = win_ref.shape[2]
    head_size = cols // heads
    weights = jnp.swapaxes(win_ref[...], 0, 1)
    normed = normed_ref[...]
    gate_ref[...] = silu(dot(normed, weights[0]))
    query = silu(dot(normed, weights[1])).astype(BF16).astype(F32)
    self_key = silu(dot(normed, weights[2]))
    spread = jnp.where(iota((heads, cols), 0) == iota((heads, cols), 1) // head_size, 1.0, 0.0)
    first_bias = jnp.sum(spread * bias_ref[:, 0:1], axis=0, keepdims=True)
    score = head_sums(query * self_key, head_size) * head_size**-0.5 + first_bias
    self_ref[...] = silu(score) * silu(dot(normed, weights[3]))
    half = wout_ref.shape[1] // 2
    low, high = wout_ref[:, :half], wout_ref[:, half:]
    second = me_ref[1] == 1
    mine_ref[...] = jnp.where(second, high, low)
    other_ref[...] = jnp.where(second, low, high)


def attend(parts, heads, stack, owners, query, line_ref, key_ref, value_ref, store):
    cols = key_ref.shape[1]
    head_size = cols // heads
    part_rows = owners * MOST
    wide = stack * head_size
    lane = iota((part_rows, wide), 1) // head_size
    for p in range(parts):
        rows = slice(p * UNIT, (p + 1) * UNIT)
        for g in range(heads // stack):
            at = slice(g * wide, (g + 1) * wide)
            part = query[p * part_rows : (p + 1) * part_rows, at]
            zero = jnp.zeros_like(part)
            stacked = jnp.concatenate([jnp.where(lane == i, part, zero) for i in range(stack)], axis=0)
            score = dot(stacked, key_ref[rows, at], NT)
            line = jnp.concatenate(
                [
                    jnp.broadcast_to(line_ref[stack * g + i : stack * g + i + 1, rows], (part_rows, UNIT))
                    for i in range(stack)
                ],
                axis=0,
            )
            t = score + line
            weight = (t + t * jnp.tanh(t)).astype(BF16)
            summed = dot(weight, value_ref[rows, at])
            kept = summed[:part_rows]
            for i in range(1, stack):
                kept = jnp.where(lane == i, summed[i * part_rows : (i + 1) * part_rows], kept)
            for k in range(owners):
                store(k, p, at, kept[k * MOST : (k + 1) * MOST])


def near_kernel(
    parts, levels, heads, stack, scale,
    me_ref, lens_ref, cand_ref, table_ref, win_ref, line_ref, key_ref, value_ref, *rest
):
    owners = cand_ref.shape[0]
    outs, (wq_ref, slot_ref, result_ref) = rest[:owners], rest[owners:]
    wq_ref[...] = jnp.swapaxes(win_ref[...], 0, 1)[1]
    sums_of(
        parts, levels, heads, stack, scale,
        me_ref, lens_ref, cand_ref, table_ref, wq_ref, line_ref, key_ref, value_ref, outs, slot_ref, result_ref,
    )


def far_kernel(
    parts, levels, heads, stack, scale,
    me_ref, lens_ref, cand_ref, table_ref, wq_ref, line_ref, key_ref, value_ref, *rest
):
    owners = cand_ref.shape[0]
    outs, (slot_ref, result_ref) = rest[:owners], rest[owners:]
    sums_of(
        parts, levels, heads, stack, scale,
        me_ref, lens_ref, cand_ref, table_ref, wq_ref, line_ref, key_ref, value_ref, outs, slot_ref, result_ref,
    )


def sums_of(
    parts, levels, heads, stack, scale,
    me_ref, lens_ref, cand_ref, table_ref, wq_ref, line_ref, key_ref, value_ref, outs, slot_ref, result_ref,
):
    owners = cand_ref.shape[0]
    query = slot_queries(parts, levels, scale, me_ref, lens_ref, cand_ref, table_ref, wq_ref, slot_ref)

    def store(k, p, at, value):
        result_ref[k, p * MOST : (p + 1) * MOST, at] = value

    attend(parts, heads, stack, owners, query, line_ref, key_ref, value_ref, store)
    for k in range(owners):
        outs[k][...] = result_ref[k].astype(BF16)


def mix_kernel(heads, turns, gate_ref, self_ref, assign_ref, scale_ref, wout_ref, *rest):
    received, (mixed_ref, send_ref) = rest[:-2], rest[-2:]
    received = [received[turns.index(m)] for m in range(len(turns), 0, -1)] + [received[-1]]
    head_size = gate_ref.shape[1] // heads
    history = dot(assign_ref[...], jnp.concatenate([r[...] for r in received], axis=0))
    attended = history * scale_ref[:, 0:1] + self_ref[...]
    centred = attended - head_sums(attended, head_size) * (1.0 / head_size)
    var = head_sums(centred * centred, head_size) * (1.0 / head_size)
    mixed = (centred * lax.rsqrt(var + 1e-05) * gate_ref[...]).astype(BF16)
    mixed_ref[...] = mixed
    send_ref[...] = dot(mixed, wout_ref[...]).astype(BF16)


def keep_kernel(mixed_ref, residual_ref, wout_ref, keep_ref):
    keep_ref[...] = residual_ref[...] + dot(mixed_ref[...], wout_ref[...])


def full(shape, dtype):
    return jax.ShapeDtypeStruct(shape, dtype)


def body(
    sem_tokens,
    cand_request,
    hist_lengths,
    hist_buckets,
    hist_keys,
    hist_values,
    code_table,
    proj_in,
    time_bias,
    proj_out,
):
    cand, levels = sem_tokens.shape
    hist, cols = hist_keys.shape
    heads = time_bias.shape[1]
    width = code_table.shape[1]
    owners = lax.axis_size("ctx")
    parts = hist // UNIT
    block = parts * MOST
    slots = owners * block
    stack = 4
    scale = 0.5 * (cols // heads) ** -0.5
    me = jnp.stack([lax.axis_index("ctx"), lax.axis_index("head")]).astype(jnp.int32)
    bias = time_bias.T
    smem = pl.BlockSpec(memory_space=pltpu.SMEM)
    vmem = pl.BlockSpec(memory_space=pltpu.VMEM)

    def swap(x, mask):
        return lax.ppermute(x, "ctx", [(i, i ^ mask) for i in range(owners)])

    def call(kernel, name, flops, out_shape, in_specs, scratch=(), cost=1 << 20):
        return pl.pallas_call(
            kernel,
            out_shape=out_shape,
            in_specs=in_specs,
            out_specs=jax.tree.map(lambda _: vmem, out_shape),
            scratch_shapes=scratch,
            compiler_params=pltpu.CompilerParams(vmem_limit_bytes=(8 + owners) << 20),
            cost_estimate=pl.CostEstimate(flops=flops, bytes_accessed=cost, transcendentals=0),
            name=name,
        )

    payload = jnp.concatenate(
        [sem_tokens.T, cand_request.T, jnp.zeros((ROWS - levels - 1, cand), jnp.int32)], axis=0
    )
    payload = call(
        payload_kernel, "payload", 9_000_000_000, full((ROWS, cand), jnp.int32), [vmem], cost=32 << 20
    )(payload)
    normed, residual, assign, lengths, line, payload_next = call(
        functools.partial(prepare_kernel, levels, heads, parts),
        "prepare",
        8_000_000_000,
        [
            full((cand, width), BF16),
            full((cand, width // 2), F32),
            full((cand, slots), BF16),
            full((cand, LANES), F32),
            full((heads, hist), F32),
            full((ROWS, cand), jnp.int32),
        ],
        [smem] * 2 + [vmem] * 4,
    )(me, hist_lengths, payload, hist_buckets.reshape(1, hist), bias, code_table)
    gathered = [jnp.stack([payload_next] + [swap(payload, m) for m in (3, 2, 1)][::-1])]
    bit = 4
    while bit < owners:
        gathered.append(jnp.concatenate([gathered[-1], swap(gathered[-1], bit)], axis=0))
        bit *= 2
    near_cand, far_cand = gathered[-2], gathered[-1][owners // 2 :]
    half = owners // 2
    scratch = [pltpu.VMEM((slots // 2, ROWS), F32), pltpu.VMEM((half, block, cols), F32)]
    *near, wq = call(
        functools.partial(near_kernel, parts, levels, heads, stack, scale),
        "near",
        1_000_000_000,
        [full((block, cols), BF16)] * half + [full((width, cols), BF16)],
        [smem] * 2 + [vmem] * 6,
        scratch,
    )(me, hist_lengths, near_cand, code_table, proj_in, line, hist_keys, hist_values)
    far = call(
        functools.partial(far_kernel, parts, levels, heads, stack, scale),
        "far",
        3_000_000_000,
        [full((block, cols), BF16)] * half,
        [smem] * 2 + [vmem] * 6,
        scratch,
    )(me, hist_lengths, far_cand, code_table, wq, line, hist_keys, hist_values)
    early = []
    late = [m for m in range(owners) if m not in early]
    sums = list(near) + list(far)
    tied = lax.optimization_barrier(tuple(sums[m] for m in late))
    sent = [tied[late.index(m)] if m in late else sums[m] for m in range(owners)]
    gate, self_term, wout_mine, wout_other = call(
        functools.partial(own_kernel, heads),
        "own",
        1_000_000_000,
        [full((cand, cols), F32)] * 2 + [full((cols, width // 2), BF16)] * 2,
        [smem] + [vmem] * 5,
    )(me, sent[0], bias, normed, proj_in, proj_out)
    turns = [4, 7, 5, 6, 3, 2, 1] if owners == 8 else list(range(owners - 1, 0, -1))
    received = [swap(sent[m], m) for m in turns] + [sent[0]]
    mixed, send = call(
        functools.partial(mix_kernel, heads, turns),
        "mix",
        1_000_000_000,
        [full((cand, cols), BF16), full((cand, width // 2), BF16)],
        [vmem] * (5 + owners),
    )(gate, self_term, assign, lengths, wout_other, *received)
    other = lax.ppermute(send, "head", [(0, 1), (1, 0)])
    keep = call(keep_kernel, "keep", 1_000_000, full((cand, width // 2), F32), [vmem] * 3)(
        mixed, residual, wout_mine
    )
    return (keep + other.astype(F32)).astype(BF16)


def solution(mesh):
    in_specs = (
        P(("groups", "ctx"), None),
        P(("groups", "ctx"), None),
        P("groups"),
        P(("groups", "ctx")),
        P(("groups", "ctx"), "head"),
        P(("groups", "ctx"), "head"),
        P(),
        P(None, None, "head"),
        P(None, "head"),
        P("head", None),
    )
    out_specs = P(("groups", "ctx"), "head")
    return jax.shard_map(body, mesh=mesh, in_specs=in_specs, out_specs=out_specs, check_vma=False)
```

```python
import functools

import jax
import jax.numpy as jnp
from jax import lax
from jax.experimental import pallas as pl
from jax.experimental.pallas import tpu as pltpu
from jax.sharding import PartitionSpec as P

MOST = 24
UNIT = 512
ROWS = 8
LANES = 128

BF16 = jnp.bfloat16
F32 = jnp.float32
NN = (((1,), (0,)), ((), ()))
NT = (((1,), (1,)), ((), ()))


def dot(a, b, dims=NN):
    return lax.dot_general(a, b, dims, preferred_element_type=F32)


def silu(v):
    t = 0.5 * v
    return t + t * jnp.tanh(t)


def iota(shape, dim):
    return lax.broadcasted_iota(jnp.int32, shape, dim)


def ones_where(mask):
    return jnp.where(mask, 1.0, 0.0).astype(BF16)


def head_sums(x, head_size):
    rows, cols = x.shape
    tall = jnp.concatenate([x[:, at : at + LANES] for at in range(0, cols, LANES)], axis=0)
    same = ones_where(iota((LANES, LANES), 0) // head_size == iota((LANES, LANES), 1) // head_size)
    high = tall.astype(BF16)
    low = (tall - high.astype(F32)).astype(BF16)
    sums = dot(high, same) + dot(low, same)
    return jnp.concatenate([sums[at : at + rows] for at in range(0, sums.shape[0], rows)], axis=1)


def request_at(position, lens_ref):
    end = lens_ref[0]
    request = jnp.where(position >= end, 1, 0)
    for r in range(1, lens_ref.shape[0]):
        end = end + lens_ref[r]
        request = request + jnp.where(position >= end, 1, 0)
    return request


def embed(tokens, levels, table):
    codes = table.shape[0] // levels
    lane = iota((tokens.shape[0], codes), 1).astype(F32)
    hot = jnp.concatenate([ones_where(lane == tokens[:, l : l + 1]) for l in range(levels)], axis=1)
    return dot(hot, table)


def normalize(embedded):
    width = embedded.shape[1]
    mean = jnp.sum(embedded, axis=1, keepdims=True) * (1.0 / width)
    centred = embedded - mean
    var = jnp.sum(centred * centred, axis=1, keepdims=True) * (1.0 / width)
    return (centred * lax.rsqrt(var + 1e-05)).astype(BF16)


def slot_queries(parts, levels, scale, target_ref, cand_ref, table_ref, wq_ref, slot_ref):
    owners, _, cand = cand_ref.shape
    order = ones_where(iota((cand, cand), 0) <= iota((cand, cand), 1))
    slot = iota((MOST, cand), 0).astype(F32) + 1.0
    requests = jnp.concatenate([cand_ref[:, levels, :]] * parts, axis=0)
    line = iota(requests.shape, 0) // owners
    target = jnp.zeros(requests.shape, jnp.int32)
    for p in range(parts):
        target = jnp.where(line == p, target_ref[p : p + 1, :], target)
    wanted = requests == target
    rank = jnp.where(wanted, dot(ones_where(wanted), order), 0.0)
    for k in range(owners):
        pick = jnp.concatenate(
            [ones_where(slot == rank[p * owners + k : p * owners + k + 1, :]) for p in range(parts)], axis=0
        )
        facts = dot(pick, cand_ref[k].astype(F32).astype(BF16), NT)
        for p in range(parts):
            at = (p * owners + k) * MOST
            slot_ref[at : at + MOST, :] = facts[p * MOST : (p + 1) * MOST]
    query = dot(normalize(embed(slot_ref[...], levels, table_ref[...])), wq_ref[...])
    return silu(query).astype(BF16) * BF16(scale)


def payload_kernel(cand_ref, out_ref):
    out_ref[...] = cand_ref[...]


def prepare_kernel(
    levels, heads, parts, me_ref, lens_ref, cand_ref, bucket_ref, bias_ref, table_ref,
    normed_ref, residual_ref, assign_ref, scale_ref, line_ref, target_ref, next_ref,
):
    _, cand = cand_ref.shape
    eye = ones_where(iota((cand, cand), 0) == iota((cand, cand), 1))
    facts = dot(eye, cand_ref[...].astype(F32).astype(BF16), NT)
    embedded = embed(facts, levels, table_ref[...])
    half = embedded.shape[1] // 2
    residual_ref[...] = jnp.where(me_ref[1] == 1, embedded[:, half:], embedded[:, :half])
    normed_ref[...] = normalize(embedded)
    buckets = bias_ref.shape[1]
    hot = ones_where(iota((buckets, bucket_ref.shape[1]), 0) == bucket_ref[...])
    bias = bias_ref[...] * 0.5
    high = bias.astype(BF16)
    low = (bias - high.astype(F32)).astype(BF16)
    line_ref[...] = dot(high, hot) + dot(low, hot)
    request = facts[:, levels : levels + 1]
    other = cand_ref[levels : levels + 1, :].astype(F32)
    before = iota((cand, cand), 0) > iota((cand, cand), 1)
    rank = jnp.sum(jnp.where(jnp.logical_and(request == other, before), 1.0, 0.0), axis=1, keepdims=True)
    line = iota((1, assign_ref.shape[1]), 1)
    block = line // MOST
    owners = assign_ref.shape[1] // (parts * MOST)
    shard = jnp.bitwise_xor(owners - 1 - block // parts, me_ref[0])
    slot_request = request_at((shard * parts + block % parts) * UNIT, lens_ref).astype(F32)
    hit = jnp.logical_and(request == slot_request, rank == (line % MOST).astype(F32))
    assign_ref[...] = ones_where(hit)
    length = jnp.zeros((cand, 1), F32)
    for r in range(lens_ref.shape[0]):
        length = jnp.where(request == float(r), lens_ref[r].astype(F32), length)
    scale_ref[...] = jnp.broadcast_to(lax.rsqrt(length), scale_ref.shape)
    row = iota(target_ref.shape, 0)
    target = jnp.where(row == target_ref.shape[0] - 1, me_ref[1], 0)
    for p in range(parts):
        target = jnp.where(row == p, request_at((me_ref[0] * parts + p) * UNIT, lens_ref), target)
    target_ref[...] = target
    next_ref[...] = cand_ref[...]


def own_kernel(
    heads, target_ref, sent_ref, bias_ref, normed_ref, win_ref, wout_ref, gate_ref, self_ref, mine_ref, other_ref
):
    cols = win_ref.shape[2]
    head_size = cols // heads
    weights = jnp.swapaxes(win_ref[...], 0, 1)
    normed = normed_ref[...]
    gate_ref[...] = silu(dot(normed, weights[0]))
    query = silu(dot(normed, weights[1])).astype(BF16).astype(F32)
    self_key = silu(dot(normed, weights[2]))
    spread = jnp.where(iota((heads, cols), 0) == iota((heads, cols), 1) // head_size, 1.0, 0.0)
    first_bias = jnp.sum(spread * bias_ref[:, 0:1], axis=0, keepdims=True)
    score = head_sums(query * self_key, head_size) * head_size**-0.5 + first_bias
    self_ref[...] = silu(score) * silu(dot(normed, weights[3]))
    half = wout_ref.shape[1] // 2
    low, high = wout_ref[:, :half], wout_ref[:, half:]
    second = target_ref[target_ref.shape[0] - 1 :, 0:1].astype(F32)
    to_high = jnp.broadcast_to(second, low.shape).astype(BF16)
    to_low = jnp.broadcast_to(1.0 - second, low.shape).astype(BF16)
    mine_ref[...] = high * to_high + low * to_low
    other_ref[...] = high * to_low + low * to_high


def attend(parts, heads, stack, owners, query, line_ref, key_ref, value_ref, store):
    cols = key_ref.shape[1]
    head_size = cols // heads
    part_rows = owners * MOST
    wide = stack * head_size
    lane = iota((part_rows, wide), 1) // head_size
    for p in range(parts):
        rows = slice(p * UNIT, (p + 1) * UNIT)
        for g in range(heads // stack):
            at = slice(g * wide, (g + 1) * wide)
            part = query[p * part_rows : (p + 1) * part_rows, at]
            zero = jnp.zeros_like(part)
            stacked = jnp.concatenate([jnp.where(lane == i, part, zero) for i in range(stack)], axis=0)
            score = dot(stacked, key_ref[rows, at], NT)
            line = jnp.concatenate(
                [
                    jnp.broadcast_to(line_ref[stack * g + i : stack * g + i + 1, rows], (part_rows, UNIT))
                    for i in range(stack)
                ],
                axis=0,
            )
            t = score + line
            weight = (t + t * jnp.tanh(t)).astype(BF16)
            summed = dot(weight, value_ref[rows, at])
            kept = summed[:part_rows]
            for i in range(1, stack):
                kept = jnp.where(lane == i, summed[i * part_rows : (i + 1) * part_rows], kept)
            for k in range(owners):
                store(k, p, at, kept[k * MOST : (k + 1) * MOST])


def near_kernel(
    parts, levels, heads, stack, scale,
    target_ref, cand_ref, table_ref, win_ref, line_ref, key_ref, value_ref, *rest
):
    owners = cand_ref.shape[0]
    outs, (wq_ref, slot_ref, result_ref) = rest[:owners], rest[owners:]
    wq_ref[...] = jnp.swapaxes(win_ref[...], 0, 1)[1]
    sums_of(
        parts, levels, heads, stack, scale,
        target_ref, cand_ref, table_ref, wq_ref, line_ref, key_ref, value_ref, outs, slot_ref, result_ref,
    )


def far_kernel(
    parts, levels, heads, stack, scale,
    target_ref, cand_ref, table_ref, wq_ref, line_ref, key_ref, value_ref, *rest
):
    owners = cand_ref.shape[0]
    outs, (slot_ref, result_ref) = rest[:owners], rest[owners:]
    sums_of(
        parts, levels, heads, stack, scale,
        target_ref, cand_ref, table_ref, wq_ref, line_ref, key_ref, value_ref, outs, slot_ref, result_ref,
    )


def sums_of(
    parts, levels, heads, stack, scale,
    target_ref, cand_ref, table_ref, wq_ref, line_ref, key_ref, value_ref, outs, slot_ref, result_ref,
):
    owners = cand_ref.shape[0]
    query = slot_queries(parts, levels, scale, target_ref, cand_ref, table_ref, wq_ref, slot_ref)

    def store(k, p, at, value):
        result_ref[k, p * MOST : (p + 1) * MOST, at] = value

    attend(parts, heads, stack, owners, query, line_ref, key_ref, value_ref, store)
    for k in range(owners):
        outs[k][...] = result_ref[k].astype(BF16)


def mix_kernel(heads, turns, gate_ref, self_ref, assign_ref, scale_ref, wout_ref, *rest):
    received, (mixed_ref, send_ref) = rest[:-2], rest[-2:]
    received = [received[turns.index(m)] for m in range(len(turns), 0, -1)] + [received[-1]]
    head_size = gate_ref.shape[1] // heads
    history = dot(assign_ref[...], jnp.concatenate([r[...] for r in received], axis=0))
    attended = history * scale_ref[:, 0:1] + self_ref[...]
    centred = attended - head_sums(attended, head_size) * (1.0 / head_size)
    var = head_sums(centred * centred, head_size) * (1.0 / head_size)
    mixed = (centred * lax.rsqrt(var + 1e-05) * gate_ref[...]).astype(BF16)
    mixed_ref[...] = mixed
    send_ref[...] = dot(mixed, wout_ref[...]).astype(BF16)


def keep_kernel(mixed_ref, residual_ref, wout_ref, keep_ref):
    keep_ref[...] = residual_ref[...] + dot(mixed_ref[...], wout_ref[...])


def full(shape, dtype):
    return jax.ShapeDtypeStruct(shape, dtype)


def body(
    sem_tokens,
    cand_request,
    hist_lengths,
    hist_buckets,
    hist_keys,
    hist_values,
    code_table,
    proj_in,
    time_bias,
    proj_out,
):
    cand, levels = sem_tokens.shape
    hist, cols = hist_keys.shape
    heads = time_bias.shape[1]
    width = code_table.shape[1]
    owners = lax.axis_size("ctx")
    parts = hist // UNIT
    block = parts * MOST
    slots = owners * block
    stack = 4
    scale = 0.5 * (cols // heads) ** -0.5
    me = jnp.stack([lax.axis_index("ctx"), lax.axis_index("head")]).astype(jnp.int32)
    bias = time_bias.T
    smem = pl.BlockSpec(memory_space=pltpu.SMEM)
    vmem = pl.BlockSpec(memory_space=pltpu.VMEM)

    def swap(x, mask):
        return lax.ppermute(x, "ctx", [(i, i ^ mask) for i in range(owners)])

    def call(kernel, name, flops, out_shape, in_specs, scratch=(), cost=1 << 20):
        return pl.pallas_call(
            kernel,
            out_shape=out_shape,
            in_specs=in_specs,
            out_specs=jax.tree.map(lambda _: vmem, out_shape),
            scratch_shapes=scratch,
            compiler_params=pltpu.CompilerParams(vmem_limit_bytes=(8 + owners) << 20),
            cost_estimate=pl.CostEstimate(flops=flops, bytes_accessed=cost, transcendentals=0),
            name=name,
        )

    payload = jnp.concatenate(
        [sem_tokens.T, cand_request.T, jnp.zeros((ROWS - levels - 1, cand), jnp.int32)], axis=0
    )
    payload = call(
        payload_kernel, "payload", 9_000_000_000, full((ROWS, cand), jnp.int32), [vmem], cost=32 << 20
    )(payload)
    normed, residual, assign, lengths, line, target, payload_next = call(
        functools.partial(prepare_kernel, levels, heads, parts),
        "prepare",
        8_000_000_000,
        [
            full((cand, width), BF16),
            full((cand, width // 2), F32),
            full((cand, slots), BF16),
            full((cand, LANES), F32),
            full((heads, hist), F32),
            full((ROWS, cand), jnp.int32),
            full((ROWS, cand), jnp.int32),
        ],
        [smem] * 2 + [vmem] * 4,
    )(me, hist_lengths, payload, hist_buckets.reshape(1, hist), bias, code_table)
    gathered = [jnp.stack([payload_next] + [swap(payload, m) for m in (3, 2, 1)][::-1])]
    bit = 4
    while bit < owners:
        gathered.append(jnp.concatenate([gathered[-1], swap(gathered[-1], bit)], axis=0))
        bit *= 2
    near_cand, far_cand = gathered[-2], gathered[-1][owners // 2 :]
    half = owners // 2
    scratch = [pltpu.VMEM((slots // 2, ROWS), F32), pltpu.VMEM((half, block, cols), F32)]
    *near, wq = call(
        functools.partial(near_kernel, parts, levels, heads, stack, scale),
        "near",
        1_000_000_000,
        [full((block, cols), BF16)] * half + [full((width, cols), BF16)],
        [vmem] * 7,
        scratch,
    )(target, near_cand, code_table, proj_in, line, hist_keys, hist_values)
    far = call(
        functools.partial(far_kernel, parts, levels, heads, stack, scale),
        "far",
        3_000_000_000,
        [full((block, cols), BF16)] * half,
        [vmem] * 7,
        scratch,
    )(target, far_cand, code_table, wq, line, hist_keys, hist_values)
    early = []
    late = [m for m in range(owners) if m not in early]
    sums = list(near) + list(far)
    tied = lax.optimization_barrier(tuple(sums[m] for m in late))
    sent = [tied[late.index(m)] if m in late else sums[m] for m in range(owners)]
    gate, self_term, wout_mine, wout_other = call(
        functools.partial(own_kernel, heads),
        "own",
        1_000_000_000,
        [full((cand, cols), F32)] * 2 + [full((cols, width // 2), BF16)] * 2,
        [vmem] * 6,
    )(target, sent[0], bias, normed, proj_in, proj_out)
    turns = [4, 7, 5, 6, 3, 2, 1] if owners == 8 else list(range(owners - 1, 0, -1))
    received = [swap(sent[m], m) for m in turns] + [sent[0]]
    mixed, send = call(
        functools.partial(mix_kernel, heads, turns),
        "mix",
        1_000_000_000,
        [full((cand, cols), BF16), full((cand, width // 2), BF16)],
        [vmem] * (5 + owners),
    )(gate, self_term, assign, lengths, wout_other, *received)
    other = lax.ppermute(send, "head", [(0, 1), (1, 0)])
    keep = call(keep_kernel, "keep", 1_000_000, full((cand, width // 2), F32), [vmem] * 3)(
        mixed, residual, wout_mine
    )
    return (keep + other.astype(F32)).astype(BF16)


def solution(mesh):
    in_specs = (
        P(("groups", "ctx"), None),
        P(("groups", "ctx"), None),
        P("groups"),
        P(("groups", "ctx")),
        P(("groups", "ctx"), "head"),
        P(("groups", "ctx"), "head"),
        P(),
        P(None, None, "head"),
        P(None, "head"),
        P("head", None),
    )
    out_specs = P(("groups", "ctx"), "head")
    return jax.shard_map(body, mesh=mesh, in_specs=in_specs, out_specs=out_specs, check_vma=False)
```

```python
import functools

import jax
import jax.numpy as jnp
from jax import lax
from jax.experimental import pallas as pl
from jax.experimental.pallas import tpu as pltpu
from jax.sharding import PartitionSpec as P

MOST = 24
UNIT = 512
ROWS = 8
LANES = 128

BF16 = jnp.bfloat16
F32 = jnp.float32
NN = (((1,), (0,)), ((), ()))
NT = (((1,), (1,)), ((), ()))


def dot(a, b, dims=NN):
    return lax.dot_general(a, b, dims, preferred_element_type=F32)


def silu(v):
    t = 0.5 * v
    return t + t * jnp.tanh(t)


def iota(shape, dim):
    return lax.broadcasted_iota(jnp.int32, shape, dim)


def ones_where(mask):
    return jnp.where(mask, 1.0, 0.0).astype(BF16)


def head_sums(x, head_size):
    rows, cols = x.shape
    tall = jnp.concatenate([x[:, at : at + LANES] for at in range(0, cols, LANES)], axis=0)
    same = ones_where(iota((LANES, LANES), 0) // head_size == iota((LANES, LANES), 1) // head_size)
    high = tall.astype(BF16)
    low = (tall - high.astype(F32)).astype(BF16)
    sums = dot(high, same) + dot(low, same)
    return jnp.concatenate([sums[at : at + rows] for at in range(0, sums.shape[0], rows)], axis=1)


def request_at(position, lens_ref):
    end = lens_ref[0]
    request = jnp.where(position >= end, 1, 0)
    for r in range(1, lens_ref.shape[0]):
        end = end + lens_ref[r]
        request = request + jnp.where(position >= end, 1, 0)
    return request


def embed(tokens, levels, table):
    codes = table.shape[0] // levels
    lane = iota((tokens.shape[0], codes), 1).astype(F32)
    hot = jnp.concatenate([ones_where(lane == tokens[:, l : l + 1]) for l in range(levels)], axis=1)
    return dot(hot, table)


def normalize(embedded):
    width = embedded.shape[1]
    mean = jnp.sum(embedded, axis=1, keepdims=True) * (1.0 / width)
    centred = embedded - mean
    var = jnp.sum(centred * centred, axis=1, keepdims=True) * (1.0 / width)
    return (centred * lax.rsqrt(var + 1e-05)).astype(BF16)


def slot_queries(parts, levels, scale, target_ref, cand_ref, table_ref, wq_ref, slot_ref):
    owners, _, cand = cand_ref.shape
    order = ones_where(iota((cand, cand), 0) <= iota((cand, cand), 1))
    slot = iota((MOST, cand), 0).astype(F32) + 1.0
    requests = jnp.concatenate([cand_ref[:, levels, :]] * parts, axis=0)
    line = iota(requests.shape, 0) // owners
    target = jnp.zeros(requests.shape, jnp.int32)
    for p in range(parts):
        target = jnp.where(line == p, target_ref[p : p + 1, :], target)
    wanted = requests == target
    rank = jnp.where(wanted, dot(ones_where(wanted), order), 0.0)
    for k in range(owners):
        pick = jnp.concatenate(
            [ones_where(slot == rank[p * owners + k : p * owners + k + 1, :]) for p in range(parts)], axis=0
        )
        facts = dot(pick, cand_ref[k].astype(F32).astype(BF16), NT)
        for p in range(parts):
            at = (p * owners + k) * MOST
            slot_ref[at : at + MOST, :] = facts[p * MOST : (p + 1) * MOST]
    query = dot(normalize(embed(slot_ref[...], levels, table_ref[...])), wq_ref[...])
    return silu(query).astype(BF16) * BF16(scale)


def payload_kernel(cand_ref, out_ref):
    out_ref[...] = cand_ref[...]


def prepare_kernel(
    levels, heads, parts, me_ref, lens_ref, cand_ref, bucket_ref, bias_ref, table_ref,
    normed_ref, residual_ref, assign_ref, scale_ref, line_ref, target_ref, next_ref,
):
    _, cand = cand_ref.shape
    eye = ones_where(iota((cand, cand), 0) == iota((cand, cand), 1))
    facts = dot(eye, cand_ref[...].astype(F32).astype(BF16), NT)
    embedded = embed(facts, levels, table_ref[...])
    half = embedded.shape[1] // 2
    residual_ref[...] = jnp.where(me_ref[1] == 1, embedded[:, half:], embedded[:, :half])
    normed_ref[...] = normalize(embedded)
    buckets = bias_ref.shape[1]
    hot = ones_where(iota((buckets, bucket_ref.shape[1]), 0) == bucket_ref[...])
    bias = bias_ref[...] * 0.5
    high = bias.astype(BF16)
    low = (bias - high.astype(F32)).astype(BF16)
    line_ref[...] = dot(high, hot) + dot(low, hot)
    request = facts[:, levels : levels + 1]
    other = cand_ref[levels : levels + 1, :].astype(F32)
    before = iota((cand, cand), 0) > iota((cand, cand), 1)
    rank = jnp.sum(jnp.where(jnp.logical_and(request == other, before), 1.0, 0.0), axis=1, keepdims=True)
    line = iota((1, assign_ref.shape[1]), 1)
    block = line // MOST
    owners = assign_ref.shape[1] // (parts * MOST)
    shard = jnp.bitwise_xor(owners - 1 - block // parts, me_ref[0])
    slot_request = request_at((shard * parts + block % parts) * UNIT, lens_ref).astype(F32)
    hit = jnp.logical_and(request == slot_request, rank == (line % MOST).astype(F32))
    assign_ref[...] = ones_where(hit)
    length = jnp.zeros((cand, 1), F32)
    for r in range(lens_ref.shape[0]):
        length = jnp.where(request == float(r), lens_ref[r].astype(F32), length)
    scale_ref[...] = jnp.broadcast_to(lax.rsqrt(length), scale_ref.shape)
    row = iota(target_ref.shape, 0)
    target = jnp.where(row == target_ref.shape[0] - 1, me_ref[1], 0)
    for p in range(parts):
        target = jnp.where(row == p, request_at((me_ref[0] * parts + p) * UNIT, lens_ref), target)
    target_ref[...] = target
    next_ref[...] = cand_ref[...]


def own_kernel(
    heads, target_ref, sent_ref, bias_ref, normed_ref, win_ref, wout_ref, gate_ref, self_ref, mine_ref, other_ref
):
    cols = win_ref.shape[2]
    head_size = cols // heads
    weights = jnp.swapaxes(win_ref[...], 0, 1)
    normed = normed_ref[...]
    gate_ref[...] = silu(dot(normed, weights[0]))
    query = silu(dot(normed, weights[1])).astype(BF16).astype(F32)
    self_key = silu(dot(normed, weights[2]))
    spread = jnp.where(iota((heads, cols), 0) == iota((heads, cols), 1) // head_size, 1.0, 0.0)
    first_bias = jnp.sum(spread * bias_ref[:, 0:1], axis=0, keepdims=True)
    score = head_sums(query * self_key, head_size) * head_size**-0.5 + first_bias
    self_ref[...] = silu(score) * silu(dot(normed, weights[3]))
    half = wout_ref.shape[1] // 2
    low, high = wout_ref[:, :half], wout_ref[:, half:]
    second = target_ref[target_ref.shape[0] - 1 :, 0:1].astype(F32)
    to_high = jnp.broadcast_to(second, low.shape).astype(BF16)
    to_low = jnp.broadcast_to(1.0 - second, low.shape).astype(BF16)
    mine_ref[...] = high * to_high + low * to_low
    other_ref[...] = high * to_low + low * to_high


def attend(parts, heads, stack, owners, query, line_ref, key_ref, value_ref, store):
    cols = key_ref.shape[1]
    head_size = cols // heads
    part_rows = owners * MOST
    wide = stack * head_size
    lane = iota((part_rows, wide), 1) // head_size
    for p in range(parts):
        rows = slice(p * UNIT, (p + 1) * UNIT)
        for g in range(heads // stack):
            at = slice(g * wide, (g + 1) * wide)
            part = query[p * part_rows : (p + 1) * part_rows, at]
            zero = jnp.zeros_like(part)
            stacked = jnp.concatenate([jnp.where(lane == i, part, zero) for i in range(stack)], axis=0)
            score = dot(stacked, key_ref[rows, at], NT)
            line = jnp.concatenate(
                [
                    jnp.broadcast_to(line_ref[stack * g + i : stack * g + i + 1, rows], (part_rows, UNIT))
                    for i in range(stack)
                ],
                axis=0,
            )
            t = score + line
            weight = (t + t * jnp.tanh(t)).astype(BF16)
            summed = dot(weight, value_ref[rows, at])
            kept = summed[:part_rows]
            for i in range(1, stack):
                kept = jnp.where(lane == i, summed[i * part_rows : (i + 1) * part_rows], kept)
            for k in range(owners):
                store(k, p, at, kept[k * MOST : (k + 1) * MOST])


def near_kernel(
    parts, levels, heads, stack, scale,
    target_ref, cand_ref, table_ref, win_ref, line_ref, key_ref, value_ref, *rest
):
    owners = cand_ref.shape[0]
    outs, (wq_ref, slot_ref, result_ref) = rest[:owners], rest[owners:]
    wq_ref[...] = jnp.swapaxes(win_ref[...], 0, 1)[1]
    sums_of(
        parts, levels, heads, stack, scale,
        target_ref, cand_ref, table_ref, wq_ref, line_ref, key_ref, value_ref, outs, slot_ref, result_ref,
    )


def far_kernel(
    parts, levels, heads, stack, scale,
    target_ref, cand_ref, table_ref, wq_ref, line_ref, key_ref, value_ref, *rest
):
    owners = cand_ref.shape[0]
    outs, (slot_ref, result_ref) = rest[:owners], rest[owners:]
    sums_of(
        parts, levels, heads, stack, scale,
        target_ref, cand_ref, table_ref, wq_ref, line_ref, key_ref, value_ref, outs, slot_ref, result_ref,
    )


def sums_of(
    parts, levels, heads, stack, scale,
    target_ref, cand_ref, table_ref, wq_ref, line_ref, key_ref, value_ref, outs, slot_ref, result_ref,
):
    owners = cand_ref.shape[0]
    query = slot_queries(parts, levels, scale, target_ref, cand_ref, table_ref, wq_ref, slot_ref)

    def store(k, p, at, value):
        result_ref[k, p * MOST : (p + 1) * MOST, at] = value

    attend(parts, heads, stack, owners, query, line_ref, key_ref, value_ref, store)
    for k in range(owners):
        outs[k][...] = result_ref[k].astype(BF16)


def mix_kernel(heads, turns, gate_ref, self_ref, assign_ref, scale_ref, wout_ref, *rest):
    received, (mixed_ref, send_ref) = rest[:-2], rest[-2:]
    received = [received[turns.index(m)] for m in range(len(turns), 0, -1)] + [received[-1]]
    head_size = gate_ref.shape[1] // heads
    history = dot(assign_ref[...], jnp.concatenate([r[...] for r in received], axis=0))
    attended = history * scale_ref[:, 0:1] + self_ref[...]
    centred = attended - head_sums(attended, head_size) * (1.0 / head_size)
    var = head_sums(centred * centred, head_size) * (1.0 / head_size)
    mixed = (centred * lax.rsqrt(var + 1e-05) * gate_ref[...]).astype(BF16)
    mixed_ref[...] = mixed
    send_ref[...] = dot(mixed, wout_ref[...]).astype(BF16)


def keep_kernel(mixed_ref, residual_ref, wout_ref, keep_ref):
    keep_ref[...] = residual_ref[...] + dot(mixed_ref[...], wout_ref[...])


def full(shape, dtype):
    return jax.ShapeDtypeStruct(shape, dtype)


def body(
    sem_tokens,
    cand_request,
    hist_lengths,
    hist_buckets,
    hist_keys,
    hist_values,
    code_table,
    proj_in,
    time_bias,
    proj_out,
):
    cand, levels = sem_tokens.shape
    hist, cols = hist_keys.shape
    heads = time_bias.shape[1]
    width = code_table.shape[1]
    owners = lax.axis_size("ctx")
    parts = hist // UNIT
    block = parts * MOST
    slots = owners * block
    stack = 4
    scale = 0.5 * (cols // heads) ** -0.5
    me = jnp.stack([lax.axis_index("ctx"), lax.axis_index("head")]).astype(jnp.int32)
    bias = time_bias.T
    smem = pl.BlockSpec(memory_space=pltpu.SMEM)
    vmem = pl.BlockSpec(memory_space=pltpu.VMEM)

    def swap(x, mask):
        return lax.ppermute(x, "ctx", [(i, i ^ mask) for i in range(owners)])

    def call(kernel, name, flops, out_shape, in_specs, scratch=(), cost=1 << 20):
        return pl.pallas_call(
            kernel,
            out_shape=out_shape,
            in_specs=in_specs,
            out_specs=jax.tree.map(lambda _: vmem, out_shape),
            scratch_shapes=scratch,
            compiler_params=pltpu.CompilerParams(vmem_limit_bytes=(8 + owners) << 20),
            cost_estimate=pl.CostEstimate(flops=flops, bytes_accessed=cost, transcendentals=0),
            name=name,
        )

    payload = jnp.concatenate(
        [sem_tokens.T, cand_request.T, jnp.zeros((ROWS - levels - 1, cand), jnp.int32)], axis=0
    )
    payload = call(
        payload_kernel, "payload", 9_000_000_000, full((ROWS, cand), jnp.int32), [vmem], cost=32 << 20
    )(payload)
    normed, residual, assign, lengths, line, target, payload_next = call(
        functools.partial(prepare_kernel, levels, heads, parts),
        "prepare",
        8_000_000_000,
        [
            full((cand, width), BF16),
            full((cand, width // 2), F32),
            full((cand, slots), BF16),
            full((cand, LANES), F32),
            full((heads, hist), F32),
            full((ROWS, cand), jnp.int32),
            full((ROWS, cand), jnp.int32),
        ],
        [smem] * 2 + [vmem] * 4,
    )(me, hist_lengths, payload, hist_buckets.reshape(1, hist), bias, code_table)
    gathered = [jnp.stack([payload_next] + [swap(payload, m) for m in (3, 2, 1)][::-1])]
    bit = 4
    while bit < owners:
        gathered.append(jnp.concatenate([gathered[-1], swap(gathered[-1], bit)], axis=0))
        bit *= 2
    near_cand, far_cand = gathered[-2], gathered[-1][owners // 2 :]
    half = owners // 2
    scratch = [pltpu.VMEM((slots // 2, ROWS), F32), pltpu.VMEM((half, block, cols), F32)]
    *near, wq = call(
        functools.partial(near_kernel, parts, levels, heads, stack, scale),
        "near",
        1_000_000_000,
        [full((block, cols), BF16)] * half + [full((width, cols), BF16)],
        [vmem] * 7,
        scratch,
    )(target, near_cand, code_table, proj_in, line, hist_keys, hist_values)
    far = call(
        functools.partial(far_kernel, parts, levels, heads, stack, scale),
        "far",
        3_000_000_000,
        [full((block, cols), BF16)] * half,
        [vmem] * 7,
        scratch,
    )(target, far_cand, code_table, wq, line, hist_keys, hist_values)
    sent = list(lax.optimization_barrier(tuple(near) + tuple(far)))
    gate, self_term, wout_mine, wout_other = call(
        functools.partial(own_kernel, heads),
        "own",
        1_000_000_000,
        [full((cand, cols), F32)] * 2 + [full((cols, width // 2), BF16)] * 2,
        [vmem] * 6,
    )(target, sent[0], bias, normed, proj_in, proj_out)
    turns = [4, 6, 5, 7, 3, 2, 1] if owners == 8 else list(range(owners - 1, 0, -1))
    received = [swap(sent[m], m) for m in turns] + [sent[0]]
    mixed, send = call(
        functools.partial(mix_kernel, heads, turns),
        "mix",
        1_000_000_000,
        [full((cand, cols), BF16), full((cand, width // 2), BF16)],
        [vmem] * (5 + owners),
    )(gate, self_term, assign, lengths, wout_other, *received)
    other = lax.ppermute(send, "head", [(0, 1), (1, 0)])
    keep = call(keep_kernel, "keep", 1_000_000, full((cand, width // 2), F32), [vmem] * 3)(
        mixed, residual, wout_mine
    )
    return (keep + other.astype(F32)).astype(BF16)


def solution(mesh):
    in_specs = (
        P(("groups", "ctx"), None),
        P(("groups", "ctx"), None),
        P("groups"),
        P(("groups", "ctx")),
        P(("groups", "ctx"), "head"),
        P(("groups", "ctx"), "head"),
        P(),
        P(None, None, "head"),
        P(None, "head"),
        P("head", None),
    )
    out_specs = P(("groups", "ctx"), "head")
    return jax.shard_map(body, mesh=mesh, in_specs=in_specs, out_specs=out_specs, check_vma=False)
```

```python
import functools

import jax
import jax.numpy as jnp
from jax import lax
from jax.experimental import pallas as pl
from jax.experimental.pallas import tpu as pltpu
from jax.sharding import PartitionSpec as P

MOST = 24
UNIT = 512
ROWS = 8
LANES = 128

BF16 = jnp.bfloat16
F32 = jnp.float32
NN = (((1,), (0,)), ((), ()))
NT = (((1,), (1,)), ((), ()))


def dot(a, b, dims=NN):
    return lax.dot_general(a, b, dims, preferred_element_type=F32)


def silu(v):
    t = 0.5 * v
    return t + t * jnp.tanh(t)


def iota(shape, dim):
    return lax.broadcasted_iota(jnp.int32, shape, dim)


def ones_where(mask):
    return jnp.where(mask, 1.0, 0.0).astype(BF16)


def head_sums(x, head_size, split=True):
    rows, cols = x.shape
    tall = jnp.concatenate([x[:, at : at + LANES] for at in range(0, cols, LANES)], axis=0)
    same = ones_where(iota((LANES, LANES), 0) // head_size == iota((LANES, LANES), 1) // head_size)
    high = tall.astype(BF16)
    sums = dot(high, same)
    if split:
        sums = sums + dot((tall - high.astype(F32)).astype(BF16), same)
    return jnp.concatenate([sums[at : at + rows] for at in range(0, sums.shape[0], rows)], axis=1)


def request_at(position, lens_ref):
    end = lens_ref[0]
    request = jnp.where(position >= end, 1, 0)
    for r in range(1, lens_ref.shape[0]):
        end = end + lens_ref[r]
        request = request + jnp.where(position >= end, 1, 0)
    return request


def embed(tokens, levels, table):
    codes = table.shape[0] // levels
    lane = iota((tokens.shape[0], codes), 1).astype(F32)
    hot = jnp.concatenate([ones_where(lane == tokens[:, l : l + 1]) for l in range(levels)], axis=1)
    return dot(hot, table)


def normalize(embedded):
    width = embedded.shape[1]
    mean = jnp.sum(embedded, axis=1, keepdims=True) * (1.0 / width)
    centred = embedded - mean
    var = jnp.sum(centred * centred, axis=1, keepdims=True) * (1.0 / width)
    return (centred * lax.rsqrt(var + 1e-05)).astype(BF16)


def slot_queries(parts, levels, scale, target_ref, cand_ref, table_ref, wq_ref, slot_ref):
    owners, _, cand = cand_ref.shape
    order = ones_where(iota((cand, cand), 0) <= iota((cand, cand), 1))
    slot = iota((MOST, cand), 0).astype(F32) + 1.0
    requests = jnp.concatenate([cand_ref[:, levels, :]] * parts, axis=0)
    line = iota(requests.shape, 0) // owners
    target = jnp.zeros(requests.shape, jnp.int32)
    for p in range(parts):
        target = jnp.where(line == p, target_ref[p : p + 1, :], target)
    wanted = requests == target
    rank = jnp.where(wanted, dot(ones_where(wanted), order), 0.0)
    for k in range(owners):
        pick = jnp.concatenate(
            [ones_where(slot == rank[p * owners + k : p * owners + k + 1, :]) for p in range(parts)], axis=0
        )
        facts = dot(pick, cand_ref[k].astype(F32).astype(BF16), NT)
        for p in range(parts):
            at = (p * owners + k) * MOST
            slot_ref[at : at + MOST, :] = facts[p * MOST : (p + 1) * MOST]
    query = dot(normalize(embed(slot_ref[...], levels, table_ref[...])), wq_ref[...])
    return silu(query).astype(BF16) * BF16(scale)


def payload_kernel(cand_ref, out_ref):
    out_ref[...] = cand_ref[...]


def prepare_kernel(
    levels, heads, parts, me_ref, lens_ref, cand_ref, bucket_ref, bias_ref, table_ref,
    normed_ref, residual_ref, assign_ref, scale_ref, line_ref, target_ref, next_ref,
):
    _, cand = cand_ref.shape
    eye = ones_where(iota((cand, cand), 0) == iota((cand, cand), 1))
    facts = dot(eye, cand_ref[...].astype(F32).astype(BF16), NT)
    embedded = embed(facts, levels, table_ref[...])
    half = embedded.shape[1] // 2
    residual_ref[...] = jnp.where(me_ref[1] == 1, embedded[:, half:], embedded[:, :half])
    normed_ref[...] = normalize(embedded)
    buckets = bias_ref.shape[1]
    hot = ones_where(iota((buckets, bucket_ref.shape[1]), 0) == bucket_ref[...])
    bias = bias_ref[...] * 0.5
    high = bias.astype(BF16)
    low = (bias - high.astype(F32)).astype(BF16)
    line_ref[...] = dot(high, hot) + dot(low, hot)
    request = facts[:, levels : levels + 1]
    other = cand_ref[levels : levels + 1, :].astype(F32)
    before = iota((cand, cand), 0) > iota((cand, cand), 1)
    rank = jnp.sum(jnp.where(jnp.logical_and(request == other, before), 1.0, 0.0), axis=1, keepdims=True)
    line = iota((1, assign_ref.shape[1]), 1)
    block = line // MOST
    owners = assign_ref.shape[1] // (parts * MOST)
    shard = jnp.bitwise_xor(owners - 1 - block // parts, me_ref[0])
    slot_request = request_at((shard * parts + block % parts) * UNIT, lens_ref).astype(F32)
    hit = jnp.logical_and(request == slot_request, rank == (line % MOST).astype(F32))
    assign_ref[...] = ones_where(hit)
    length = jnp.zeros((cand, 1), F32)
    for r in range(lens_ref.shape[0]):
        length = jnp.where(request == float(r), lens_ref[r].astype(F32), length)
    scale_ref[...] = jnp.broadcast_to(lax.rsqrt(length), scale_ref.shape)
    row = iota(target_ref.shape, 0)
    target = jnp.where(row == target_ref.shape[0] - 1, me_ref[1], 0)
    for p in range(parts):
        target = jnp.where(row == p, request_at((me_ref[0] * parts + p) * UNIT, lens_ref), target)
    target_ref[...] = target
    next_ref[...] = cand_ref[...]


def own_kernel(
    heads, target_ref, sent_ref, bias_ref, normed_ref, win_ref, wout_ref, gate_ref, self_ref, mine_ref, other_ref
):
    cols = win_ref.shape[2]
    head_size = cols // heads
    weights = jnp.swapaxes(win_ref[...], 0, 1)
    normed = normed_ref[...]
    gate_ref[...] = silu(dot(normed, weights[0]))
    query = silu(dot(normed, weights[1])).astype(BF16).astype(F32)
    self_key = silu(dot(normed, weights[2]))
    spread = jnp.where(iota((heads, cols), 0) == iota((heads, cols), 1) // head_size, 1.0, 0.0)
    first_bias = jnp.sum(spread * bias_ref[:, 0:1], axis=0, keepdims=True)
    score = head_sums(query * self_key, head_size) * head_size**-0.5 + first_bias
    self_ref[...] = silu(score) * silu(dot(normed, weights[3]))
    half = wout_ref.shape[1] // 2
    low, high = wout_ref[:, :half], wout_ref[:, half:]
    second = target_ref[target_ref.shape[0] - 1 :, 0:1].astype(F32)
    to_high = jnp.broadcast_to(second, low.shape).astype(BF16)
    to_low = jnp.broadcast_to(1.0 - second, low.shape).astype(BF16)
    mine_ref[...] = high * to_high + low * to_low
    other_ref[...] = high * to_low + low * to_high


def attend(parts, heads, stack, owners, query, line_ref, key_ref, value_ref, store):
    cols = key_ref.shape[1]
    head_size = cols // heads
    part_rows = owners * MOST
    wide = stack * head_size
    lane = iota((part_rows, wide), 1) // head_size
    for p in range(parts):
        rows = slice(p * UNIT, (p + 1) * UNIT)
        for g in range(heads // stack):
            at = slice(g * wide, (g + 1) * wide)
            part = query[p * part_rows : (p + 1) * part_rows, at]
            zero = jnp.zeros_like(part)
            stacked = jnp.concatenate([jnp.where(lane == i, part, zero) for i in range(stack)], axis=0)
            score = dot(stacked, key_ref[rows, at], NT)
            line = jnp.concatenate(
                [
                    jnp.broadcast_to(line_ref[stack * g + i : stack * g + i + 1, rows], (part_rows, UNIT))
                    for i in range(stack)
                ],
                axis=0,
            )
            t = score + line
            weight = (t + t * jnp.tanh(t)).astype(BF16)
            summed = dot(weight, value_ref[rows, at])
            kept = summed[:part_rows]
            for i in range(1, stack):
                kept = jnp.where(lane == i, summed[i * part_rows : (i + 1) * part_rows], kept)
            for k in range(owners):
                store(k, p, at, kept[k * MOST : (k + 1) * MOST])


def near_kernel(
    parts, levels, heads, stack, scale,
    target_ref, cand_ref, table_ref, win_ref, line_ref, key_ref, value_ref, *rest
):
    owners = cand_ref.shape[0]
    outs, (wq_ref, slot_ref, result_ref) = rest[:owners], rest[owners:]
    wq_ref[...] = jnp.swapaxes(win_ref[...], 0, 1)[1]
    sums_of(
        parts, levels, heads, stack, scale,
        target_ref, cand_ref, table_ref, wq_ref, line_ref, key_ref, value_ref, outs, slot_ref, result_ref,
    )


def far_kernel(
    parts, levels, heads, stack, scale,
    target_ref, cand_ref, table_ref, wq_ref, line_ref, key_ref, value_ref, *rest
):
    owners = cand_ref.shape[0]
    outs, (slot_ref, result_ref) = rest[:owners], rest[owners:]
    sums_of(
        parts, levels, heads, stack, scale,
        target_ref, cand_ref, table_ref, wq_ref, line_ref, key_ref, value_ref, outs, slot_ref, result_ref,
    )


def sums_of(
    parts, levels, heads, stack, scale,
    target_ref, cand_ref, table_ref, wq_ref, line_ref, key_ref, value_ref, outs, slot_ref, result_ref,
):
    owners = cand_ref.shape[0]
    query = slot_queries(parts, levels, scale, target_ref, cand_ref, table_ref, wq_ref, slot_ref)

    def store(k, p, at, value):
        result_ref[k, p * MOST : (p + 1) * MOST, at] = value

    attend(parts, heads, stack, owners, query, line_ref, key_ref, value_ref, store)
    for k in range(owners):
        outs[k][...] = result_ref[k].astype(BF16)


def mix_kernel(heads, turns, gate_ref, self_ref, assign_ref, scale_ref, wout_ref, *rest):
    received, (mixed_ref, send_ref) = rest[:-2], rest[-2:]
    received = [received[turns.index(m)] for m in range(len(turns), 0, -1)] + [received[-1]]
    head_size = gate_ref.shape[1] // heads
    history = dot(assign_ref[...], jnp.concatenate([r[...] for r in received], axis=0))
    attended = history * scale_ref[:, 0:1] + self_ref[...]
    centred = attended - head_sums(attended, head_size) * (1.0 / head_size)
    var = head_sums(centred * centred, head_size, split=False) * (1.0 / head_size)
    mixed = (centred * lax.rsqrt(var + 1e-05) * gate_ref[...]).astype(BF16)
    mixed_ref[...] = mixed
    send_ref[...] = dot(mixed, wout_ref[...]).astype(BF16)


def keep_kernel(mixed_ref, residual_ref, wout_ref, keep_ref):
    keep_ref[...] = residual_ref[...] + dot(mixed_ref[...], wout_ref[...])


def full(shape, dtype):
    return jax.ShapeDtypeStruct(shape, dtype)


def body(
    sem_tokens,
    cand_request,
    hist_lengths,
    hist_buckets,
    hist_keys,
    hist_values,
    code_table,
    proj_in,
    time_bias,
    proj_out,
):
    cand, levels = sem_tokens.shape
    hist, cols = hist_keys.shape
    heads = time_bias.shape[1]
    width = code_table.shape[1]
    owners = lax.axis_size("ctx")
    parts = hist // UNIT
    block = parts * MOST
    slots = owners * block
    stack = 4
    scale = 0.5 * (cols // heads) ** -0.5
    me = jnp.stack([lax.axis_index("ctx"), lax.axis_index("head")]).astype(jnp.int32)
    bias = time_bias.T
    smem = pl.BlockSpec(memory_space=pltpu.SMEM)
    vmem = pl.BlockSpec(memory_space=pltpu.VMEM)

    def swap(x, mask):
        return lax.ppermute(x, "ctx", [(i, i ^ mask) for i in range(owners)])

    def call(kernel, name, flops, out_shape, in_specs, scratch=(), cost=1 << 20):
        return pl.pallas_call(
            kernel,
            out_shape=out_shape,
            in_specs=in_specs,
            out_specs=jax.tree.map(lambda _: vmem, out_shape),
            scratch_shapes=scratch,
            compiler_params=pltpu.CompilerParams(vmem_limit_bytes=(8 + owners) << 20),
            cost_estimate=pl.CostEstimate(flops=flops, bytes_accessed=cost, transcendentals=0),
            name=name,
        )

    payload = jnp.concatenate(
        [sem_tokens.T, cand_request.T, jnp.zeros((ROWS - levels - 1, cand), jnp.int32)], axis=0
    )
    payload = call(
        payload_kernel, "payload", 9_000_000_000, full((ROWS, cand), jnp.int32), [vmem], cost=32 << 20
    )(payload)
    normed, residual, assign, lengths, line, target, payload_next = call(
        functools.partial(prepare_kernel, levels, heads, parts),
        "prepare",
        8_000_000_000,
        [
            full((cand, width), BF16),
            full((cand, width // 2), F32),
            full((cand, slots), BF16),
            full((cand, LANES), F32),
            full((heads, hist), F32),
            full((ROWS, cand), jnp.int32),
            full((ROWS, cand), jnp.int32),
        ],
        [smem] * 2 + [vmem] * 4,
    )(me, hist_lengths, payload, hist_buckets.reshape(1, hist), bias, code_table)
    gathered = [jnp.stack([payload_next] + [swap(payload, m) for m in (3, 2, 1)][::-1])]
    bit = 4
    while bit < owners:
        gathered.append(jnp.concatenate([gathered[-1], swap(gathered[-1], bit)], axis=0))
        bit *= 2
    near_cand, far_cand = gathered[-2], gathered[-1][owners // 2 :]
    half = owners // 2
    scratch = [pltpu.VMEM((slots // 2, ROWS), F32), pltpu.VMEM((half, block, cols), F32)]
    *near, wq = call(
        functools.partial(near_kernel, parts, levels, heads, stack, scale),
        "near",
        1_000_000_000,
        [full((block, cols), BF16)] * half + [full((width, cols), BF16)],
        [vmem] * 7,
        scratch,
    )(target, near_cand, code_table, proj_in, line, hist_keys, hist_values)
    far = call(
        functools.partial(far_kernel, parts, levels, heads, stack, scale),
        "far",
        3_000_000_000,
        [full((block, cols), BF16)] * half,
        [vmem] * 7,
        scratch,
    )(target, far_cand, code_table, wq, line, hist_keys, hist_values)
    sent = list(lax.optimization_barrier(tuple(near) + tuple(far)))
    gate, self_term, wout_mine, wout_other = call(
        functools.partial(own_kernel, heads),
        "own",
        1_000_000_000,
        [full((cand, cols), F32)] * 2 + [full((cols, width // 2), BF16)] * 2,
        [vmem] * 6,
    )(target, sent[0], bias, normed, proj_in, proj_out)
    turns = [4, 6, 5, 7, 3, 2, 1] if owners == 8 else list(range(owners - 1, 0, -1))
    received = [swap(sent[m], m) for m in turns] + [sent[0]]
    mixed, send = call(
        functools.partial(mix_kernel, heads, turns),
        "mix",
        1_000_000_000,
        [full((cand, cols), BF16), full((cand, width // 2), BF16)],
        [vmem] * (5 + owners),
    )(gate, self_term, assign, lengths, wout_other, *received)
    other = lax.ppermute(send, "head", [(0, 1), (1, 0)])
    keep = call(keep_kernel, "keep", 1_000_000, full((cand, width // 2), F32), [vmem] * 3)(
        mixed, residual, wout_mine
    )
    return (keep + other.astype(F32)).astype(BF16)


def solution(mesh):
    in_specs = (
        P(("groups", "ctx"), None),
        P(("groups", "ctx"), None),
        P("groups"),
        P(("groups", "ctx")),
        P(("groups", "ctx"), "head"),
        P(("groups", "ctx"), "head"),
        P(),
        P(None, None, "head"),
        P(None, "head"),
        P("head", None),
    )
    out_specs = P(("groups", "ctx"), "head")
    return jax.shard_map(body, mesh=mesh, in_specs=in_specs, out_specs=out_specs, check_vma=False)
```
